512 devices in a mesh: tm: 128 (over z, x_lo, y), space: 4 (over x_hi, core).
Axes of the slice: x: 4 (x_hi: 2, x_lo: 2; x = x_hi * 2 + x_lo), y: 4, z: 16, core: 2. Of those that a mesh axis runs over, the one named last changes fastest.
Arguments:
- initial_state: float32 [64, 1024], P(None, 'space'), may hold values from -4 to 4
- inv_mass: float32 [1024], P('space'), may hold values from 0.5 to 1
- element_scale: float32 [1024], P('space'), may hold values from 0.7 to 1.4
- mode_rate: float32 [128, 64], P('tm'), may hold values from 0.0005 to 1.2
- volume_block: bfloat16 [64, 64], replicated, may hold values from -0.0046 to 0.0016
- face_blocks: bfloat16 [6, 64, 64], replicated, may hold values from -0.0016 to 0.0046
Outputs:
- slice_end: float32 [128, 64, 1024], P('tm', None, 'space')
- first_guess: float32 [128, 64, 1024], P('tm', None, 'space')
The draws below stay inside these ranges and needn't reach their ends.
All inputs are finite; a program needn't handle non-finite values.
Results may differ from the reference program's by a relative error of at most 0.0003.
Values may be sent and summed in bfloat16 or wider, within the bound.
A program may use at most 64 MiB of HBM per device.

```python
import math
import jax
import jax.numpy as jnp
from jax import lax

DOF = 64
EY = 16
EZ = 8
FINE = 8
ITERS = 2
TIME_SLICES = 128
ELEMS = 1024


def draw_initial_state(key, part):
    return jnp.clip(jax.random.normal(key, (DOF, ELEMS), jnp.float32), -4.0, 4.0)


def draw_mode_rate(key, part):
    random_keys = jax.random.split(key, 6)
    fast_share = 0.5
    fast_mode = jax.random.bernoulli(random_keys[0], fast_share, (DOF,))
    fast_rate = jax.random.uniform(random_keys[1], (DOF,), jnp.float32, 0.05, 0.08)
    slow_rate = jax.random.uniform(random_keys[2], (DOF,), jnp.float32, 0.001, 0.003)
    baseline_rate = jnp.where(fast_mode, fast_rate, slow_rate)
    random_wobble = jnp.exp(jax.random.uniform(random_keys[3], (TIME_SLICES, DOF), jnp.float32, -0.5, 0.35))
    spiking_slices = jax.random.randint(random_keys[4], (2,), 0, TIME_SLICES)
    spike_magnitude = jax.random.uniform(random_keys[5], (2,), jnp.float32, 0.22, 0.5)
    slice_numbers = jnp.arange(TIME_SLICES)
    spike_hits = (slice_numbers[:, None] == spiking_slices[None, :]).astype(jnp.float32)
    spike_events = jnp.sum(spike_hits * spike_magnitude[None, :], axis=1)
    return baseline_rate[None, :] * random_wobble + spike_events[:, None]


def random_part(key, shape):
    return jnp.clip(jax.random.normal(key, shape, jnp.float32), -4.0, 4.0)


def draw_volume_block(key, part):
    identity = jnp.eye(DOF, dtype=jnp.float32)
    values = -0.003 * identity + 0.003 * DOF ** (-0.5) * random_part(key, (DOF, DOF))
    return values.astype(jnp.bfloat16)


def draw_face_blocks(key, part):
    identity = jnp.eye(DOF, dtype=jnp.float32)
    diagonal_part = jnp.array([0.003, 0.001, 0.001, 0.001, 0.001, 0.001], jnp.float32)
    values = diagonal_part[:, None, None] * identity[None] + 0.003 * DOF ** (-0.5) * random_part(key, (6, DOF, DOF))
    return values.astype(jnp.bfloat16)


def level_of(own_key, shape, cuts, least, top_value):
    level, own = 1.0, jax.random.fold_in(own_key, 6)
    for position, shards_of in cuts:
        steps = jnp.exp(jax.random.uniform(jax.random.fold_in(own, position), (shards_of,), jnp.float32, least / len(cuts), top_value / len(cuts)))
        level = level * jnp.repeat(steps, shape[position] // shards_of).reshape([-1 if axis == position else 1 for axis in range(len(shape))])
    return level


def setup_inputs(seed: int = 0) -> dict:
    keys = jax.random.split(jax.random.key(seed), 7)
    initial_state = draw_initial_state(jax.random.fold_in(keys[6], 71), 0)
    inv_mass = jnp.clip(jnp.exp(math.log(1.0) - 0.6931472 * jax.random.uniform(keys[1], (ELEMS,), jnp.float32) ** level_of(keys[1], (ELEMS,), ((0, 4),), -0.2, 0.2)), 0.5, 1.0)
    element_scale = jnp.clip(jnp.exp(math.log(1.4) - 0.6931472 * jax.random.uniform(keys[2], (ELEMS,), jnp.float32) ** level_of(keys[2], (ELEMS,), ((0, 4),), -0.2, 0.2)), 0.7, 1.4)
    mode_rate = draw_mode_rate(jax.random.fold_in(keys[6], 71), 0)
    volume_block = draw_volume_block(jax.random.fold_in(keys[6], 71), 0)
    face_blocks = draw_face_blocks(jax.random.fold_in(keys[6], 71), 0)
    return dict(initial_state=initial_state, inv_mass=inv_mass, element_scale=element_scale, mode_rate=mode_rate, volume_block=volume_block, face_blocks=face_blocks)


def operator_terms(padded, all_blocks):
    layer_size = EY * EZ
    cell_count = padded.shape[1] - 2 * layer_size
    centre = padded[:, layer_size:layer_size + cell_count]
    behind = padded[:, :cell_count]
    in_front = padded[:, 2 * layer_size:]
    shaped = centre.reshape(DOF, cell_count // layer_size, EY, EZ)
    south_side = jnp.roll(shaped, 1, axis=2).reshape(DOF, cell_count)
    north_side = jnp.roll(shaped, -1, axis=2).reshape(DOF, cell_count)
    lower_side = jnp.roll(shaped, 1, axis=3).reshape(DOF, cell_count)
    upper_side = jnp.roll(shaped, -1, axis=3).reshape(DOF, cell_count)
    stacked = jnp.concatenate([centre, behind, in_front, south_side, north_side, lower_side, upper_side], axis=0)
    return jnp.dot(all_blocks, stacked, preferred_element_type=jnp.float32)


def reference(initial_state, inv_mass, element_scale, mode_rate, volume_block, face_blocks):
    mass_row = inv_mass[None, :]
    all_blocks = jnp.concatenate([volume_block] + [face_blocks[face_index] for face_index in range(6)], axis=1)

    def slice_offset(inputs):
        slice_start, rate_row = inputs
        scaled = rate_row[:, None] * element_scale[None, :]
        slice_decay = jnp.exp(-scaled)
        step_decay = jnp.exp(-scaled / FINE)
        fine_state = slice_start
        zero_edge = jnp.zeros((DOF, EY * EZ), jnp.bfloat16)
        for fine_step in range(FINE):
            rounded = fine_state.astype(jnp.bfloat16)
            padded = jnp.concatenate([zero_edge, rounded, zero_edge], axis=1)
            fine_state = step_decay * fine_state + mass_row * operator_terms(padded, all_blocks)
        return fine_state - slice_decay * slice_start

    def advance(carried, inputs):
        offset, rate_row = inputs
        slice_decay = jnp.exp(-(rate_row[:, None] * element_scale[None, :]))
        following = slice_decay * carried + offset
        return following, following

    summed_rates = jnp.cumsum(mode_rate, axis=0)
    passed = jnp.concatenate([jnp.zeros((1, DOF), jnp.float32), summed_rates[:-1]], axis=0)
    slice_starts = jnp.exp(-(passed[:, :, None] * element_scale[None, None, :])) * initial_state[None]
    first_guess = slice_starts
    endings = slice_starts
    for sweep_index in range(ITERS):
        offsets = lax.map(slice_offset, (slice_starts, mode_rate))
        ignored, endings = lax.scan(advance, initial_state, (offsets, mode_rate))
        slice_starts = jnp.concatenate([initial_state[None], endings[:-1]], axis=0)
    return (endings, first_guess)
```

```python
import functools

import jax
import jax.numpy as jnp
from jax import lax
from jax.experimental import pallas as pl
from jax.experimental.pallas import tpu as pltpu
from jax.sharding import PartitionSpec as P

DOF = 64
EY = 16
EZ = 8
FINE = 8
ITERS = 2
LAYER = EY * EZ
MESH = pl.DeviceIdType.MESH


def kernel(
    depth, plane, shards,
    init_ref, mass_ref, scale_ref, rate_ref, volume_ref, faces_ref,
    end_ref, guess_ref,
    blocks, state, decay, coarse, start, rounded, full, halo, rows, row_src,
    rate_src, plane_rates, tot_src, z_rates,
    plane_gain, z_gain, off_src, offs, sum_src, sums, back_src, back,
    rate_send, rate_recv, tot_send, tot_recv, halo_send, halo_recv, row_send, row_recv,
    off_send, off_recv, sum_send, sum_recv, back_send, back_recv,
):
    group = DOF // plane
    cells = init_ref.shape[1]
    time = lax.axis_index("tm")
    mine = lax.axis_index("space")
    z = time // plane
    j = lax.rem(time, plane)

    def plane_peer(q):
        return (z * plane + q, mine)

    def z_peer(k):
        return (k * plane + j, mine)

    def space_peer(p):
        return (time, p)

    def others(count, me, body):
        def step(d, carry):
            body(lax.rem(me + 1 + d, count))
            return carry

        lax.fori_loop(0, count - 1, step, 0)

    barrier = pltpu.get_barrier_semaphore()
    others(plane, j, lambda q: pl.semaphore_signal(barrier, inc=1, device_id=plane_peer(q), device_id_type=MESH))
    others(shards, mine, lambda p: pl.semaphore_signal(barrier, inc=1, device_id=space_peer(p), device_id_type=MESH))
    others(depth, z, lambda k: pl.semaphore_signal(barrier, inc=1, device_id=z_peer(k), device_id_type=MESH))

    blocks[:, :DOF] = volume_ref[...]
    for f in range(6):
        blocks[:, DOF * (f + 1) : DOF * (f + 2)] = faces_ref[f]
    zero_half = jnp.zeros((DOF, cells), jnp.bfloat16)
    rounded[0] = zero_half
    rounded[shards + 1] = zero_half
    row = jnp.concatenate([rate_ref[...], jnp.zeros((1, 128 - DOF), jnp.float32)], axis=1)
    rate_src[...] = row
    plane_rates[pl.ds(j, 1)] = row[None]
    row_src[...] = jnp.concatenate(
        [mass_ref[...], scale_ref[...], jnp.zeros((6, cells), jnp.float32)], axis=0
    )
    rows[pl.ds(mine, 1)] = row_src[...][None]
    full[pl.ds(mine, 1)] = init_ref[...][None]
    sub = lax.broadcasted_iota(jnp.int32, (DOF, 128), 0)
    lane = lax.broadcasted_iota(jnp.int32, (DOF, 128), 1)
    sub_g = lax.broadcasted_iota(jnp.int32, (group, 128), 0)
    lane_g = lax.broadcasted_iota(jnp.int32, (group, 128), 1)

    def column(values):
        return jnp.sum(jnp.where(sub == lane, values, 0.0), axis=1, keepdims=True)

    def group_column(values):
        return jnp.sum(jnp.where(lane_g == sub_g + group * j, values, 0.0), axis=1, keepdims=True)

    own_scale = scale_ref[...]
    own_column = column(row)
    coarse[...] = jnp.exp(-(own_column * own_scale))

    pl.semaphore_wait(barrier, plane + shards + depth - 3)

    def rate_copy(q):
        return pltpu.make_async_remote_copy(
            src_ref=rate_src, dst_ref=plane_rates.at[j], send_sem=rate_send.at[q], recv_sem=rate_recv.at[j],
            device_id=plane_peer(q), device_id_type=MESH)

    def rate_arrival(q):
        return pltpu.make_async_remote_copy(
            src_ref=rate_src, dst_ref=plane_rates.at[q], send_sem=rate_send.at[q], recv_sem=rate_recv.at[q],
            device_id=plane_peer(q), device_id_type=MESH)

    def full_copy(p, slot):
        return pltpu.make_async_remote_copy(
            src_ref=init_ref, dst_ref=full.at[slot], send_sem=halo_send.at[0, p],
            recv_sem=halo_recv.at[0, slot], device_id=space_peer(p), device_id_type=MESH)

    def halo_copy(it, p, slot):
        return pltpu.make_async_remote_copy(
            src_ref=halo.at[it - 1, mine], dst_ref=halo.at[it - 1, slot], send_sem=halo_send.at[it, p],
            recv_sem=halo_recv.at[it, slot], device_id=space_peer(p), device_id_type=MESH)

    def row_copy(p, slot):
        return pltpu.make_async_remote_copy(
            src_ref=row_src, dst_ref=rows.at[slot], send_sem=row_send.at[p],
            recv_sem=row_recv.at[slot], device_id=space_peer(p), device_id_type=MESH)

    others(plane, j, lambda q: rate_copy(q).start())
    others(shards, mine, lambda p: row_copy(p, mine).start())
    others(shards, mine, lambda p: full_copy(p, mine).start())
    others(plane, j, lambda q: rate_arrival(q).wait_recv())
    total = jnp.zeros((1, 128), jnp.float32)
    before = jnp.zeros((1, 128), jnp.float32)
    for q in range(plane):
        before = before + jnp.where(q < j, plane_rates[q], 0.0)
        total = total + plane_rates[q]
    tot_src[...] = total

    def tot_copy(k, slot):
        return pltpu.make_async_remote_copy(
            src_ref=tot_src, dst_ref=z_rates.at[slot], send_sem=tot_send.at[k], recv_sem=tot_recv.at[slot],
            device_id=z_peer(k), device_id_type=MESH)

    def later(body):
        lax.fori_loop(0, depth - 1 - z, lambda d, c: (body(depth - 1 - d), c)[1], 0)

    later(lambda k: tot_copy(k, z).start())

    for q in range(plane):
        plane_gain[q] = jnp.exp(-(group_column(plane_rates[q]) * own_scale))
    others(shards, mine, lambda p: row_copy(p, p).wait_recv())
    for p in range(shards):
        decay[p] = jnp.exp(-(own_column * rows[p, 1:2, :]) / FINE)
    others(shards, mine, lambda p: full_copy(p, p).wait_recv())

    def add_total(k, carried):
        tot_copy(k, k).wait_recv()
        return carried + z_rates[k]

    passed = column(lax.fori_loop(0, z, add_total, before))
    for p in range(shards):
        state[p] = jnp.exp(-(passed * rows[p, 1:2, :])) * full[p]
    guess = jnp.exp(-(passed * own_scale)) * init_ref[...]
    guess_ref[...] = guess
    start[...] = guess
    state[pl.ds(mine, 1)] = guess[None]

    lane_z = lax.rem(lax.broadcasted_iota(jnp.int32, (2 * DOF, LAYER), 1), EZ)
    at_low = lane_z == 0
    at_high = lane_z == EZ - 1

    def fine_step(step, carry):
        for p in range(shards):
            rounded[p + 1] = state[p].astype(jnp.bfloat16)
        for p in range(shards):
            centre = rounded[p + 1]
            behind = jnp.concatenate([rounded[p, :, LAYER:], rounded[p + 1, :, :LAYER]], axis=1)
            ahead = jnp.concatenate([rounded[p + 1, :, LAYER:], rounded[p + 2, :, :LAYER]], axis=1)
            tall = jnp.concatenate([state[p, :, :LAYER], state[p, :, LAYER:]], axis=0)
            south = pltpu.roll(tall, EZ, 1)
            north = pltpu.roll(tall, LAYER - EZ, 1)
            lower = jnp.where(at_low, pltpu.roll(tall, LAYER - EZ + 1, 1), pltpu.roll(tall, 1, 1))
            upper = jnp.where(at_high, pltpu.roll(tall, EZ - 1, 1), pltpu.roll(tall, LAYER - 1, 1))

            def wide(value):
                value = value.astype(jnp.bfloat16)
                return jnp.concatenate([value[:DOF], value[DOF:]], axis=1)

            stacked = jnp.concatenate(
                [centre, behind, ahead, wide(south), wide(north), wide(lower), wide(upper)], axis=0
            )
            change = jnp.dot(blocks[...], stacked, preferred_element_type=jnp.float32)
            state[p] = decay[p] * state[p] + rows[p, 0:1, :] * change
        return carry

    offset = None
    for it in range(ITERS):
        lax.fori_loop(0, FINE, fine_step, 0)
        offset = state[pl.ds(mine, 1)][0] - coarse[...] * start[...]
        for q in range(plane):
            off_src[q] = offset[q * group : (q + 1) * group]

        def off_copy(q, slot):
            return pltpu.make_async_remote_copy(
                src_ref=off_src.at[q], dst_ref=offs.at[it, slot], send_sem=off_send.at[it, q],
                recv_sem=off_recv.at[it, slot], device_id=plane_peer(q), device_id_type=MESH)

        others(plane, j, lambda q: off_copy(q, j).start())
        offs[it, pl.ds(j, 1)] = off_src[pl.ds(j, 1)]
        if it == 0:
            def fill_gain(k, carry):
                z_gain[k] = jnp.exp(-(group_column(z_rates[k]) * own_scale))
                return carry

            lax.fori_loop(0, z, fill_gain, 0)
        others(plane, j, lambda q: off_copy(q, q).wait_recv())
        part = offs[it, 0]
        for q in range(1, plane):
            part = plane_gain[q] * part + offs[it, q]
        sum_src[it] = part

        def sum_copy(k, slot):
            return pltpu.make_async_remote_copy(
                src_ref=sum_src.at[it], dst_ref=sums.at[it, slot], send_sem=sum_send.at[it, k],
                recv_sem=sum_recv.at[it, slot], device_id=z_peer(k), device_id_type=MESH)

        later(lambda k: sum_copy(k, z).start())

        def add_sum(k, carried):
            sum_copy(k, k).wait_recv()
            return z_gain[k] * carried + sums[it, k]

        carried = lax.fori_loop(0, z, add_sum, jnp.zeros((group, cells), jnp.float32))
        for q in range(plane):
            back_src[it, q] = carried
            carried = plane_gain[q] * carried + offs[it, q]

        def back_copy(q, slot):
            return pltpu.make_async_remote_copy(
                src_ref=back_src.at[it, q], dst_ref=back.at[it, slot], send_sem=back_send.at[it, q],
                recv_sem=back_recv.at[it, slot], device_id=plane_peer(q), device_id_type=MESH)

        others(plane, j, lambda q: back_copy(q, j).start())
        back[it, pl.ds(j, 1)] = back_src[it, pl.ds(j, 1)]
        others(plane, j, lambda q: off_copy(q, j).wait_send())
        later(lambda k: sum_copy(k, z).wait_send())
        others(plane, j, lambda q: back_copy(q, q).wait_recv())
        following = guess_ref[...] + back[it].reshape(DOF, cells)
        if it + 1 < ITERS:
            start[...] = following
            halo[it, pl.ds(mine, 1)] = following.astype(jnp.bfloat16)[None]
            others(shards, mine, lambda p: halo_copy(it + 1, p, mine).start())
            others(shards, mine, lambda p: halo_copy(it + 1, p, p).wait_recv())
            for p in range(shards):
                state[p] = halo[it, p].astype(jnp.float32)
            state[pl.ds(mine, 1)] = following[None]
        else:
            end_ref[...] = coarse[...] * following + offset
        others(plane, j, lambda q: back_copy(q, j).wait_send())

    others(plane, j, lambda q: rate_copy(q).wait_send())
    others(shards, mine, lambda p: row_copy(p, mine).wait_send())
    others(shards, mine, lambda p: full_copy(p, mine).wait_send())
    for it in range(1, ITERS):
        others(shards, mine, lambda p: halo_copy(it, p, mine).wait_send())
    later(lambda k: tot_copy(k, z).wait_send())


def per_device(depth, plane, initial_state, inv_mass, element_scale, mode_rate, volume_block, face_blocks):
    shards = lax.axis_size("space")
    cells = initial_state.shape[1]
    group = DOF // plane
    f32, bf16 = jnp.float32, jnp.bfloat16
    vmem = pl.BlockSpec(memory_space=pltpu.VMEM)
    dma = pltpu.SemaphoreType.DMA
    end, guess = pl.pallas_call(
        functools.partial(kernel, depth, plane, shards),
        out_shape=[jax.ShapeDtypeStruct((DOF, cells), f32)] * 2,
        in_specs=[vmem] * 6,
        out_specs=[vmem] * 2,
        scratch_shapes=[
            pltpu.VMEM((DOF, 7 * DOF), bf16),
            pltpu.VMEM((shards, DOF, cells), f32),
            pltpu.VMEM((shards, DOF, cells), f32),
            pltpu.VMEM((DOF, cells), f32),
            pltpu.VMEM((DOF, cells), f32),
            pltpu.VMEM((shards + 2, DOF, cells), bf16),
            pltpu.VMEM((shards, DOF, cells), f32),
            pltpu.VMEM((ITERS - 1, shards, DOF, cells), bf16),
            pltpu.VMEM((shards, 8, cells), f32),
            pltpu.VMEM((8, cells), f32),
            pltpu.VMEM((1, 128), f32),
            pltpu.VMEM((plane, 1, 128), f32),
            pltpu.VMEM((1, 128), f32),
            pltpu.VMEM((depth, 1, 128), f32),
            pltpu.VMEM((plane, group, cells), f32),
            pltpu.VMEM((depth, group, cells), f32),
            pltpu.VMEM((plane, group, cells), f32),
            pltpu.VMEM((ITERS, plane, group, cells), f32),
            pltpu.VMEM((ITERS, group, cells), f32),
            pltpu.VMEM((ITERS, depth, group, cells), f32),
            pltpu.VMEM((ITERS, plane, group, cells), f32),
            pltpu.VMEM((ITERS, plane, group, cells), f32),
            dma((plane,)), dma((plane,)), dma((depth,)), dma((depth,)),
            dma((ITERS, shards)), dma((ITERS, shards)), dma((shards,)), dma((shards,)),
            dma((ITERS, plane)), dma((ITERS, plane)), dma((ITERS, depth)), dma((ITERS, depth)),
            dma((ITERS, plane)), dma((ITERS, plane)),
        ],
        compiler_params=pltpu.CompilerParams(collective_id=1, has_side_effects=True, vmem_limit_bytes=32 << 20),
        name="parareal",
    )(initial_state, inv_mass[None], element_scale[None], mode_rate, volume_block, face_blocks)
    return end[None], guess[None]


def solution(mesh):
    slices = mesh.shape["tm"]
    plane = 8 if slices % 8 == 0 else 2
    placed = (P(None, "space"), P("space"), P("space"), P("tm", None), P(), P())
    return jax.shard_map(
        functools.partial(per_device, slices // plane, plane),
        mesh=mesh,
        in_specs=placed,
        out_specs=(P("tm", None, "space"), P("tm", None, "space")),
        check_vma=False,
    )
```

```python
import functools

import jax
import jax.numpy as jnp
from jax import lax
from jax.experimental import pallas as pl
from jax.experimental.pallas import tpu as pltpu
from jax.sharding import PartitionSpec as P

DOF = 64
EY = 16
EZ = 8
FINE = 8
ITERS = 2
LAYER = EY * EZ
OCTET = 8
MESH = pl.DeviceIdType.MESH


def kernel(
    depth, group, shards,
    init_hbm, mass_hbm, scale_hbm, rate_hbm, volume_hbm, faces_hbm,
    end_ref, guess_ref,
    init_ref, mass_ref, scale_ref, rate_ref, volume_ref, faces_ref,
    blocks, state, decay, coarse, start, rounded, full, halo, rows, row_src,
    rate_src, group_rates, tot_src, z_rates,
    group_gain, z_gain, off_src, offs, sum_src, sums, back_src, back,
    load, rate_send, rate_recv, tot_send, tot_recv, full_send, full_recv, halo_send, halo_recv,
    row_send, row_recv, off_send, off_recv, sum_send, sum_recv, back_send, back_recv,
):
    cells = init_ref.shape[1]
    time = lax.axis_index("tm")
    mine = lax.axis_index("space")
    z = time // group
    j = lax.rem(time, group)

    def group_peer(q):
        return (z * group + q, mine)

    def z_peer(k):
        return (k * group + j, mine)

    def space_peer(p):
        return (time, p)

    def others(count, me, body):
        def step(d, carry):
            body(lax.rem(me + 1 + d, count))
            return carry

        lax.fori_loop(0, count - 1, step, 0)

    def later(body):
        lax.fori_loop(0, depth - 1 - z, lambda d, c: (body(depth - 1 - d), c)[1], 0)

    def greet(peer):
        pl.semaphore_signal(barrier, inc=1, device_id=peer, device_id_type=MESH)

    def arrived(ref, sem):
        pltpu.make_async_copy(ref, ref, sem).wait()

    barrier = pltpu.get_barrier_semaphore()
    lax.fori_loop(0, z, lambda k, c: (greet(z_peer(k)), c)[1], 0)
    others(group, j, lambda q: greet(group_peer(q)))
    others(shards, mine, lambda p: greet(space_peer(p)))

    loads = [
        pltpu.make_async_copy(src, dst, load.at[n])
        for n, (src, dst) in enumerate([
            (rate_hbm, rate_ref), (scale_hbm, scale_ref), (mass_hbm, mass_ref),
            (init_hbm, init_ref), (volume_hbm, volume_ref), (faces_hbm, faces_ref),
        ])
    ]
    for copy in loads:
        copy.start()

    zero_part = jnp.zeros((DOF, cells), jnp.bfloat16)
    rounded[0] = zero_part
    rounded[shards + 1] = zero_part
    sub = lax.broadcasted_iota(jnp.int32, (DOF, 128), 0)
    lane = lax.broadcasted_iota(jnp.int32, (DOF, 128), 1)
    sub_o = lax.broadcasted_iota(jnp.int32, (OCTET, 128), 0)
    lane_o = lax.broadcasted_iota(jnp.int32, (OCTET, 128), 1)
    first_mode = OCTET * (j // 2)

    def column(values):
        return jnp.sum(jnp.where(sub == lane, values, 0.0), axis=1, keepdims=True)

    def octet_column(values):
        return jnp.sum(jnp.where(lane_o == sub_o + first_mode, values, 0.0), axis=1, keepdims=True)

    for copy in loads:
        copy.wait()
    row = jnp.concatenate([rate_ref[...], jnp.zeros((1, 128 - DOF), jnp.float32)], axis=1)
    rate_src[...] = row
    group_rates[pl.ds(j, 1)] = row[None]
    row_src[...] = jnp.concatenate(
        [mass_ref[...], scale_ref[...], jnp.zeros((6, cells), jnp.float32)], axis=0
    )
    rows[pl.ds(mine, 1)] = row_src[...][None]
    full[pl.ds(mine, 1)] = init_ref[...][None]
    blocks[:, :DOF] = volume_ref[...]
    for f in range(6):
        blocks[:, DOF * (f + 1) : DOF * (f + 2)] = faces_ref[f]
    own_scale = scale_ref[...]
    half_scale = scale_ref[:, pl.ds(pl.multiple_of(LAYER * lax.rem(j, 2), LAYER), LAYER)]
    own_column = column(row)
    coarse[...] = jnp.exp(-(own_column * own_scale))

    pl.semaphore_wait(barrier, group + shards + depth - 3 - z)

    def rate_copy(q):
        return pltpu.make_async_remote_copy(
            src_ref=rate_src, dst_ref=group_rates.at[j], send_sem=rate_send, recv_sem=rate_recv,
            device_id=group_peer(q), device_id_type=MESH)

    def full_copy(p):
        return pltpu.make_async_remote_copy(
            src_ref=init_ref, dst_ref=full.at[mine], send_sem=full_send, recv_sem=full_recv,
            device_id=space_peer(p), device_id_type=MESH)

    def halo_copy(it, p):
        return pltpu.make_async_remote_copy(
            src_ref=halo.at[it, mine], dst_ref=halo.at[it, mine], send_sem=halo_send.at[it],
            recv_sem=halo_recv.at[it], device_id=space_peer(p), device_id_type=MESH)

    def row_copy(p):
        return pltpu.make_async_remote_copy(
            src_ref=row_src, dst_ref=rows.at[mine], send_sem=row_send, recv_sem=row_recv,
            device_id=space_peer(p), device_id_type=MESH)

    others(group, j, lambda q: rate_copy(q).start())
    others(shards, mine, lambda p: row_copy(p).start())
    others(shards, mine, lambda p: full_copy(p).start())
    arrived(group_rates.at[pl.ds(0, group - 1)], rate_recv)
    total = jnp.zeros((1, 128), jnp.float32)
    before = jnp.zeros((1, 128), jnp.float32)
    for q in range(group):
        before = before + jnp.where(q < j, group_rates[q], 0.0)
        total = total + group_rates[q]
    tot_src[...] = total

    def tot_copy(k, slot):
        return pltpu.make_async_remote_copy(
            src_ref=tot_src, dst_ref=z_rates.at[slot], send_sem=tot_send.at[k], recv_sem=tot_recv.at[slot],
            device_id=z_peer(k), device_id_type=MESH)

    later(lambda k: tot_copy(k, z).start())

    for q in range(group):
        group_gain[q] = jnp.exp(-(octet_column(group_rates[q]) * half_scale))
    arrived(rows.at[pl.ds(0, shards - 1)], row_recv)
    for p in range(shards):
        decay[p] = jnp.exp(-(own_column * rows[p, 1:2, :]) / FINE)
    arrived(full.at[pl.ds(0, shards - 1)], full_recv)

    def add_total(k, carried):
        tot_copy(k, k).wait_recv()
        return carried + z_rates[k]

    passed = column(lax.fori_loop(0, z, add_total, before))
    for p in range(shards):
        state[p] = jnp.exp(-(passed * rows[p, 1:2, :])) * full[p]
    guess = state[pl.ds(mine, 1)][0]
    guess_ref[...] = guess
    start[...] = guess

    lane_t = lax.broadcasted_iota(jnp.int32, (2 * DOF, LAYER), 1)
    lane_z = lax.rem(lane_t, EZ)
    lower_of = lane_t - lane_z + lax.rem(lane_z + EZ - 1, EZ)
    upper_of = lane_t - lane_z + lax.rem(lane_z + 1, EZ)

    def fine_step(step, carry):
        for p in range(shards):
            rounded[p + 1] = state[p].astype(jnp.bfloat16)
        for p in range(shards):
            centre = rounded[p + 1]
            behind = jnp.concatenate([rounded[p, :, LAYER:], rounded[p + 1, :, :LAYER]], axis=1)
            ahead = jnp.concatenate([rounded[p + 1, :, LAYER:], rounded[p + 2, :, :LAYER]], axis=1)
            tall = jnp.concatenate([state[p, :, :LAYER], state[p, :, LAYER:]], axis=0)
            south = pltpu.roll(tall, EZ, 1)
            north = pltpu.roll(tall, LAYER - EZ, 1)
            lower = jnp.take_along_axis(tall, lower_of, axis=1, mode="promise_in_bounds")
            upper = jnp.take_along_axis(tall, upper_of, axis=1, mode="promise_in_bounds")

            def wide(value):
                value = value.astype(jnp.bfloat16)
                return jnp.concatenate([value[:DOF], value[DOF:]], axis=1)

            stacked = jnp.concatenate(
                [centre, behind, ahead, wide(south), wide(north), wide(lower), wide(upper)], axis=0
            )
            change = jnp.dot(blocks[...], stacked, preferred_element_type=jnp.float32)
            state[p] = decay[p] * state[p] + rows[p, 0:1, :] * change
        return carry

    offset = None
    for it in range(ITERS):
        lax.fori_loop(0, FINE, fine_step, 0, unroll=FINE)
        offset = state[pl.ds(mine, 1)][0] - coarse[...] * start[...]
        for q in range(group):
            off_src[it, q] = offset[OCTET * (q // 2) : OCTET * (q // 2 + 1), LAYER * (q % 2) : LAYER * (q % 2 + 1)]

        def off_copy(q):
            return pltpu.make_async_remote_copy(
                src_ref=off_src.at[it, q], dst_ref=offs.at[it, j], send_sem=off_send.at[it],
                recv_sem=off_recv.at[it], device_id=group_peer(q), device_id_type=MESH)

        others(group, j, lambda q: off_copy(q).start())
        offs[it, pl.ds(j, 1)] = off_src[it, pl.ds(j, 1)]
        if it == 0:
            def fill_gain(k, carry):
                z_gain[k] = jnp.exp(-(octet_column(z_rates[k]) * half_scale))
                return carry

            lax.fori_loop(0, z, fill_gain, 0)
        arrived(offs.at[it, pl.ds(0, group - 1)], off_recv.at[it])
        part = offs[it, 0]
        for q in range(1, group):
            part = group_gain[q] * part + offs[it, q]
        sum_src[it] = part

        def sum_copy(k, slot):
            return pltpu.make_async_remote_copy(
                src_ref=sum_src.at[it], dst_ref=sums.at[it, slot], send_sem=sum_send.at[it, k],
                recv_sem=sum_recv.at[it, slot], device_id=z_peer(k), device_id_type=MESH)

        later(lambda k: sum_copy(k, z).start())

        def add_sum(k, carried):
            sum_copy(k, k).wait_recv()
            return z_gain[k] * carried + sums[it, k]

        carried = lax.fori_loop(0, z, add_sum, jnp.zeros((OCTET, LAYER), jnp.float32))
        for q in range(group):
            back_src[it, q] = carried
            carried = group_gain[q] * carried + offs[it, q]

        def back_copy(q):
            return pltpu.make_async_remote_copy(
                src_ref=back_src.at[it, q], dst_ref=back.at[it, j], send_sem=back_send.at[it],
                recv_sem=back_recv.at[it], device_id=group_peer(q), device_id_type=MESH)

        others(group, j, lambda q: back_copy(q).start())
        back[it, pl.ds(j, 1)] = back_src[it, pl.ds(j, 1)]
        arrived(back.at[it, pl.ds(0, group - 1)], back_recv.at[it])
        correction = jnp.concatenate(
            [jnp.concatenate([back[it, 2 * m], back[it, 2 * m + 1]], axis=1) for m in range(DOF // OCTET)], axis=0
        )
        following = guess_ref[...] + correction
        if it + 1 < ITERS:
            start[...] = following
            halo[it, pl.ds(mine, 1)] = following.astype(jnp.bfloat16)[None]
            others(shards, mine, lambda p: halo_copy(it, p).start())
            arrived(halo.at[it, pl.ds(0, shards - 1)], halo_recv.at[it])
            for p in range(shards):
                state[p] = halo[it, p].astype(jnp.float32)
            state[pl.ds(mine, 1)] = following[None]
        else:
            end_ref[...] = coarse[...] * following + offset

    def left(ref, sem):
        pltpu.make_async_copy(ref, ref, sem).wait()

    left(group_rates.at[pl.ds(0, group - 1)], rate_send)
    left(rows.at[pl.ds(0, shards - 1)], row_send)
    left(full.at[pl.ds(0, shards - 1)], full_send)
    later(lambda k: tot_copy(k, z).wait_send())
    for it in range(ITERS):
        left(off_src.at[it, pl.ds(0, group - 1)], off_send.at[it])
        left(back_src.at[it, pl.ds(0, group - 1)], back_send.at[it])
        if it + 1 < ITERS:
            left(halo.at[it, pl.ds(0, shards - 1)], halo_send.at[it])

        def summed(k):
            pltpu.make_async_copy(sum_src.at[it], sum_src.at[it], sum_send.at[it, k]).wait()

        later(summed)


def per_device(depth, group, initial_state, inv_mass, element_scale, mode_rate, volume_block, face_blocks):
    shards = lax.axis_size("space")
    cells = initial_state.shape[1]
    f32, bf16 = jnp.float32, jnp.bfloat16
    vmem = pl.BlockSpec(memory_space=pltpu.VMEM)
    hbm = pl.BlockSpec(memory_space=pltpu.HBM)
    dma = pltpu.SemaphoreType.DMA
    end, guess = pl.pallas_call(
        functools.partial(kernel, depth, group, shards),
        out_shape=[jax.ShapeDtypeStruct((DOF, cells), f32)] * 2,
        in_specs=[hbm] * 6,
        out_specs=[vmem] * 2,
        scratch_shapes=[
            pltpu.VMEM((DOF, cells), f32),
            pltpu.VMEM((1, cells), f32),
            pltpu.VMEM((1, cells), f32),
            pltpu.VMEM((1, DOF), f32),
            pltpu.VMEM((DOF, DOF), bf16),
            pltpu.VMEM((6, DOF, DOF), bf16),
            pltpu.VMEM((DOF, 7 * DOF), bf16),
            pltpu.VMEM((shards, DOF, cells), f32),
            pltpu.VMEM((shards, DOF, cells), f32),
            pltpu.VMEM((DOF, cells), f32),
            pltpu.VMEM((DOF, cells), f32),
            pltpu.VMEM((shards + 2, DOF, cells), bf16),
            pltpu.VMEM((shards, DOF, cells), f32),
            pltpu.VMEM((ITERS - 1, shards, DOF, cells), bf16),
            pltpu.VMEM((shards, 8, cells), f32),
            pltpu.VMEM((8, cells), f32),
            pltpu.VMEM((1, 128), f32),
            pltpu.VMEM((group, 1, 128), f32),
            pltpu.VMEM((1, 128), f32),
            pltpu.VMEM((depth, 1, 128), f32),
            pltpu.VMEM((group, OCTET, LAYER), f32),
            pltpu.VMEM((depth, OCTET, LAYER), f32),
            pltpu.VMEM((ITERS, group, OCTET, LAYER), f32),
            pltpu.VMEM((ITERS, group, OCTET, LAYER), f32),
            pltpu.VMEM((ITERS, OCTET, LAYER), f32),
            pltpu.VMEM((ITERS, depth, OCTET, LAYER), f32),
            pltpu.VMEM((ITERS, group, OCTET, LAYER), f32),
            pltpu.VMEM((ITERS, group, OCTET, LAYER), f32),
            dma((6,)), dma, dma, dma((depth,)), dma((depth,)),
            dma, dma, dma((ITERS,)), dma((ITERS,)),
            dma, dma, dma((ITERS,)), dma((ITERS,)),
            dma((ITERS, depth)), dma((ITERS, depth)), dma((ITERS,)), dma((ITERS,)),
        ],
        compiler_params=pltpu.CompilerParams(collective_id=1, has_side_effects=True),
        name="parareal",
    )(initial_state, inv_mass[None], element_scale[None], mode_rate, volume_block, face_blocks)
    return end[None], guess[None]


def solution(mesh):
    slices = mesh.shape["tm"]
    group = (DOF // OCTET) * 2
    placed = (P(None, "space"), P("space"), P("space"), P("tm", None), P(), P())
    return jax.shard_map(
        functools.partial(per_device, slices // group, group),
        mesh=mesh,
        in_specs=placed,
        out_specs=(P("tm", None, "space"), P("tm", None, "space")),
        check_vma=False,
    )
```

```python
import functools

import jax
import jax.numpy as jnp
from jax import lax
from jax.experimental import pallas as pl
from jax.experimental.pallas import tpu as pltpu
from jax.sharding import PartitionSpec as P

DOF = 64
EY = 16
EZ = 8
FINE = 8
ITERS = 2
LAYER = EY * EZ
OCTET = 8
NEAR = 2
MESH = pl.DeviceIdType.MESH


def kernel(
    depth, group, shards,
    init_hbm, mass_hbm, scale_hbm, rate_hbm, volume_hbm, faces_hbm,
    sum_ref, difference_ref,
    init_ref, mass_ref, scale_ref, rate_ref, volume_ref, faces_ref,
    blocks, state, decay, coarse, guess_at, start, rounded, full, halo, rows, row_src,
    rate_src, group_rates, tot_src, z_rates, pre_src, pre_dst,
    group_gain, z_gain, off_src, offs, sum_src, sums, back_src, back,
    load, ready, rate_send, rate_recv, tot_send, tot_recv, pre_send, pre_recv, full_send, full_recv, halo_send, halo_recv,
    row_send, row_recv, off_send, off_recv, sum_send, sum_recv, back_send, back_recv,
):
    cells = init_ref.shape[1]
    time = lax.axis_index("tm")
    mine = lax.axis_index("space")
    z = time // group
    j = lax.rem(time, group)

    def group_peer(q):
        return (z * group + q, mine)

    def z_peer(k):
        return (k * group + j, mine)

    def space_peer(p):
        return (time, p)

    def others(count, me, body):
        def step(d, carry):
            body(lax.rem(me + 1 + d, count))
            return carry

        lax.fori_loop(0, count - 1, step, 0)

    def later(body):
        lax.fori_loop(0, depth - 1 - z, lambda d, c: (body(depth - 1 - d), c)[1], 0)

    def greet(peer):
        pl.semaphore_signal(barrier, inc=1, device_id=peer, device_id_type=MESH)

    def arrived(ref, sem):
        pltpu.make_async_copy(ref, ref, sem).wait()

    barrier = pltpu.get_barrier_semaphore()
    last_near = jnp.minimum(z + NEAR, depth - 1)
    others(group, j, lambda q: greet(group_peer(q)))
    others(shards, mine, lambda p: greet(space_peer(p)))
    later(lambda k: greet(z_peer(k)))

    loads = [
        pltpu.make_async_copy(src, dst, load.at[n])
        for n, (src, dst) in enumerate([
            (rate_hbm, rate_ref), (scale_hbm, scale_ref), (mass_hbm, mass_ref),
            (init_hbm, init_ref), (volume_hbm, volume_ref), (faces_hbm, faces_ref),
        ])
    ]
    for copy in loads:
        copy.start()

    zero_part = jnp.zeros((DOF, cells), jnp.bfloat16)
    rounded[0] = zero_part
    rounded[shards + 1] = zero_part
    sub = lax.broadcasted_iota(jnp.int32, (DOF, 128), 0)
    lane = lax.broadcasted_iota(jnp.int32, (DOF, 128), 1)
    sub_o = lax.broadcasted_iota(jnp.int32, (OCTET, 128), 0)
    lane_o = lax.broadcasted_iota(jnp.int32, (OCTET, 128), 1)
    first_mode = OCTET * (j // 2)

    def column(values):
        return jnp.sum(jnp.where(sub == lane, values, 0.0), axis=1, keepdims=True)

    def octet_column(values):
        return jnp.sum(jnp.where(lane_o == sub_o + first_mode, values, 0.0), axis=1, keepdims=True)

    for copy in loads:
        copy.wait()
    row = jnp.concatenate([rate_ref[...], jnp.zeros((1, 128 - DOF), jnp.float32)], axis=1)
    rate_src[...] = row
    group_rates[pl.ds(j, 1)] = row[None]
    row_src[...] = jnp.concatenate(
        [mass_ref[...], scale_ref[...], jnp.zeros((6, cells), jnp.float32)], axis=0
    )
    rows[pl.ds(mine, 1)] = row_src[...][None]
    full[pl.ds(mine, 1)] = init_ref[...][None]
    blocks[:, :DOF] = volume_ref[...]
    for f in range(6):
        blocks[:, DOF * (f + 1) : DOF * (f + 2)] = faces_ref[f]
    own_scale = scale_ref[...]
    half_scale = scale_ref[:, pl.ds(pl.multiple_of(LAYER * lax.rem(j, 2), LAYER), LAYER)]
    own_column = column(row)
    coarse[...] = jnp.exp(-(own_column * own_scale))

    pl.semaphore_wait(barrier, group + shards - 2 + z)

    def rate_copy(q):
        return pltpu.make_async_remote_copy(
            src_ref=rate_src, dst_ref=group_rates.at[j], send_sem=rate_send, recv_sem=rate_recv,
            device_id=group_peer(q), device_id_type=MESH)

    def full_copy(p):
        return pltpu.make_async_remote_copy(
            src_ref=init_ref, dst_ref=full.at[mine], send_sem=full_send, recv_sem=full_recv,
            device_id=space_peer(p), device_id_type=MESH)

    def halo_copy(it, p):
        return pltpu.make_async_remote_copy(
            src_ref=halo.at[it, mine], dst_ref=halo.at[it, mine], send_sem=halo_send.at[it],
            recv_sem=halo_recv.at[it], device_id=space_peer(p), device_id_type=MESH)

    def row_copy(p):
        return pltpu.make_async_remote_copy(
            src_ref=row_src, dst_ref=rows.at[mine], send_sem=row_send, recv_sem=row_recv,
            device_id=space_peer(p), device_id_type=MESH)

    others(group, j, lambda q: rate_copy(q).start())
    lax.fori_loop(
        0, z,
        lambda k, c: (
            pl.semaphore_signal(ready.at[z], inc=1, device_id=z_peer(z - 1 - k), device_id_type=MESH), c)[1], 0)
    others(shards, mine, lambda p: row_copy(p).start())
    others(shards, mine, lambda p: full_copy(p).start())
    arrived(group_rates.at[pl.ds(0, group - 1)], rate_recv)
    total = jnp.zeros((1, 128), jnp.float32)
    before = jnp.zeros((1, 128), jnp.float32)
    for q in range(group):
        before = before + jnp.where(q < j, group_rates[q], 0.0)
        total = total + group_rates[q]
    tot_src[...] = total

    def tot_copy(k, slot):
        return pltpu.make_async_remote_copy(
            src_ref=tot_src, dst_ref=z_rates.at[slot], send_sem=tot_send.at[k], recv_sem=tot_recv.at[slot],
            device_id=z_peer(k), device_id_type=MESH)

    def tell(k, carry):
        pl.semaphore_wait(ready.at[k], 1)
        tot_copy(k, z).start()
        return carry

    lax.fori_loop(z + 1, jnp.minimum(z + 2, depth), tell, 0)

    for q in range(group):
        group_gain[q] = jnp.exp(-(octet_column(group_rates[q]) * half_scale))
    arrived(rows.at[pl.ds(0, shards - 1)], row_recv)
    for p in range(shards):
        decay[p] = jnp.exp(-(own_column * rows[p, 1:2, :]) / FINE)
    arrived(full.at[pl.ds(0, shards - 1)], full_recv)

    def pre_copy():
        return pltpu.make_async_remote_copy(
            src_ref=pre_src, dst_ref=pre_dst, send_sem=pre_send, recv_sem=pre_recv,
            device_id=z_peer(last_near), device_id_type=MESH)

    lax.fori_loop(z + 2, last_near + 1, tell, 0)

    pre_src[...] = jnp.zeros((1, 128), jnp.float32)

    @pl.when(z >= NEAR)
    def _():
        pre_copy().wait_recv()
        pre_src[...] = pre_dst[...]

    def add_total(k, carried):
        tot_copy(k, k).wait_recv()
        return carried + z_rates[k]

    ahead_of = lax.fori_loop(jnp.maximum(z - NEAR + 1, 0), z, add_total, pre_src[...])
    pre_src[...] = ahead_of + total

    @pl.when(z + NEAR < depth)
    def _():
        pre_copy().start()

    passed = column(ahead_of + before)
    for p in range(shards):
        state[p] = jnp.exp(-(passed * rows[p, 1:2, :])) * full[p]
    guess = state[pl.ds(mine, 1)][0]
    guess_at[...] = guess
    start[...] = guess

    lane_t = lax.broadcasted_iota(jnp.int32, (2 * DOF, LAYER), 1)
    lane_z = lax.rem(lane_t, EZ)
    lower_of = lane_t - lane_z + lax.rem(lane_z + EZ - 1, EZ)
    upper_of = lane_t - lane_z + lax.rem(lane_z + 1, EZ)

    def fine_step(step, carry):
        for p in range(shards):
            rounded[p + 1] = state[p].astype(jnp.bfloat16)
        for p in range(shards):
            centre = rounded[p + 1]
            behind = jnp.concatenate([rounded[p, :, LAYER:], rounded[p + 1, :, :LAYER]], axis=1)
            ahead = jnp.concatenate([rounded[p + 1, :, LAYER:], rounded[p + 2, :, :LAYER]], axis=1)
            tall = jnp.concatenate([state[p, :, :LAYER], state[p, :, LAYER:]], axis=0)
            south = pltpu.roll(tall, EZ, 1)
            north = pltpu.roll(tall, LAYER - EZ, 1)
            lower = jnp.take_along_axis(tall, lower_of, axis=1, mode="promise_in_bounds")
            upper = jnp.take_along_axis(tall, upper_of, axis=1, mode="promise_in_bounds")

            def wide(value):
                value = value.astype(jnp.bfloat16)
                return jnp.concatenate([value[:DOF], value[DOF:]], axis=1)

            stacked = jnp.concatenate(
                [centre, behind, ahead, wide(south), wide(north), wide(lower), wide(upper)], axis=0
            )
            change = jnp.dot(blocks[...], stacked, preferred_element_type=jnp.float32)
            state[p] = decay[p] * state[p] + rows[p, 0:1, :] * change
        return carry

    offset = None
    for it in range(ITERS):
        lax.fori_loop(0, FINE, fine_step, 0, unroll=FINE)
        offset = state[pl.ds(mine, 1)][0] - coarse[...] * start[...]
        for q in range(group):
            off_src[it, q] = offset[OCTET * (q // 2) : OCTET * (q // 2 + 1), LAYER * (q % 2) : LAYER * (q % 2 + 1)]

        def off_copy(q):
            return pltpu.make_async_remote_copy(
                src_ref=off_src.at[it, q], dst_ref=offs.at[it, j], send_sem=off_send.at[it],
                recv_sem=off_recv.at[it], device_id=group_peer(q), device_id_type=MESH)

        others(group, j, lambda q: off_copy(q).start())
        offs[it, pl.ds(j, 1)] = off_src[it, pl.ds(j, 1)]
        if it == 0:
            lax.fori_loop(last_near + 1, depth, tell, 0)

            def hear(k, carry):
                tot_copy(k, k).wait_recv()
                return carry

            lax.fori_loop(0, jnp.maximum(z - NEAR + 1, 0), hear, 0)

            def fill_gain(k, carry):
                z_gain[k] = jnp.exp(-(octet_column(z_rates[k]) * half_scale))
                return carry

            lax.fori_loop(0, z, fill_gain, 0)
        arrived(offs.at[it, pl.ds(0, group - 1)], off_recv.at[it])
        part = offs[it, 0]
        for q in range(1, group):
            part = group_gain[q] * part + offs[it, q]
        sum_src[it] = part

        def sum_copy(k, slot):
            return pltpu.make_async_remote_copy(
                src_ref=sum_src.at[it], dst_ref=sums.at[it, slot], send_sem=sum_send.at[it, k],
                recv_sem=sum_recv.at[it, slot], device_id=z_peer(k), device_id_type=MESH)

        later(lambda k: sum_copy(k, z).start())

        def add_sum(k, carried):
            sum_copy(k, k).wait_recv()
            return z_gain[k] * carried + sums[it, k]

        carried = lax.fori_loop(0, z, add_sum, jnp.zeros((OCTET, LAYER), jnp.float32))
        for q in range(group):
            back_src[it, q] = carried
            carried = group_gain[q] * carried + offs[it, q]

        def back_copy(q):
            return pltpu.make_async_remote_copy(
                src_ref=back_src.at[it, q], dst_ref=back.at[it, j], send_sem=back_send.at[it],
                recv_sem=back_recv.at[it], device_id=group_peer(q), device_id_type=MESH)

        others(group, j, lambda q: back_copy(q).start())
        back[it, pl.ds(j, 1)] = back_src[it, pl.ds(j, 1)]
        arrived(back.at[it, pl.ds(0, group - 1)], back_recv.at[it])
        correction = jnp.concatenate(
            [jnp.concatenate([back[it, 2 * m], back[it, 2 * m + 1]], axis=1) for m in range(DOF // OCTET)], axis=0
        )
        following = guess_at[...] + correction
        if it + 1 < ITERS:
            start[...] = following
            halo[it, pl.ds(mine, 1)] = following.astype(jnp.bfloat16)[None]
            others(shards, mine, lambda p: halo_copy(it, p).start())
            arrived(halo.at[it, pl.ds(0, shards - 1)], halo_recv.at[it])
            for p in range(shards):
                state[p] = halo[it, p].astype(jnp.float32)
            state[pl.ds(mine, 1)] = following[None]
        else:
            end = 0.5 * (coarse[...] * following + offset)
            sum_ref[...] = end + 0.5 * guess_at[...]
            difference_ref[...] = end - 0.5 * guess_at[...]

    def left(ref, sem):
        pltpu.make_async_copy(ref, ref, sem).wait()

    left(group_rates.at[pl.ds(0, group - 1)], rate_send)
    left(rows.at[pl.ds(0, shards - 1)], row_send)
    left(full.at[pl.ds(0, shards - 1)], full_send)
    later(lambda k: tot_copy(k, z).wait_send())

    @pl.when(z + NEAR < depth)
    def _():
        pre_copy().wait_send()

    for it in range(ITERS):
        left(off_src.at[it, pl.ds(0, group - 1)], off_send.at[it])
        left(back_src.at[it, pl.ds(0, group - 1)], back_send.at[it])
        if it + 1 < ITERS:
            left(halo.at[it, pl.ds(0, shards - 1)], halo_send.at[it])

        def summed(k):
            pltpu.make_async_copy(sum_src.at[it], sum_src.at[it], sum_send.at[it, k]).wait()

        later(summed)


def per_device(depth, group, initial_state, inv_mass, element_scale, mode_rate, volume_block, face_blocks):
    shards = lax.axis_size("space")
    cells = initial_state.shape[1]
    f32, bf16 = jnp.float32, jnp.bfloat16
    vmem = pl.BlockSpec(memory_space=pltpu.VMEM)
    hbm = pl.BlockSpec(memory_space=pltpu.HBM)
    dma = pltpu.SemaphoreType.DMA
    half_sum, half_difference = pl.pallas_call(
        functools.partial(kernel, depth, group, shards),
        out_shape=[pltpu.VMEM((DOF, cells), f32)] * 2,
        in_specs=[hbm] * 6,
        out_specs=[vmem] * 2,
        scratch_shapes=[
            pltpu.VMEM((DOF, cells), f32),
            pltpu.VMEM((1, cells), f32),
            pltpu.VMEM((1, cells), f32),
            pltpu.VMEM((1, DOF), f32),
            pltpu.VMEM((DOF, DOF), bf16),
            pltpu.VMEM((6, DOF, DOF), bf16),
            pltpu.VMEM((DOF, 7 * DOF), bf16),
            pltpu.VMEM((shards, DOF, cells), f32),
            pltpu.VMEM((shards, DOF, cells), f32),
            pltpu.VMEM((DOF, cells), f32),
            pltpu.VMEM((DOF, cells), f32),
            pltpu.VMEM((DOF, cells), f32),
            pltpu.VMEM((shards + 2, DOF, cells), bf16),
            pltpu.VMEM((shards, DOF, cells), f32),
            pltpu.VMEM((ITERS - 1, shards, DOF, cells), bf16),
            pltpu.VMEM((shards, 8, cells), f32),
            pltpu.VMEM((8, cells), f32),
            pltpu.VMEM((1, 128), f32),
            pltpu.VMEM((group, 1, 128), f32),
            pltpu.VMEM((1, 128), f32),
            pltpu.VMEM((depth, 1, 128), f32),
            pltpu.VMEM((1, 128), f32),
            pltpu.VMEM((1, 128), f32),
            pltpu.VMEM((group, OCTET, LAYER), f32),
            pltpu.VMEM((depth, OCTET, LAYER), f32),
            pltpu.VMEM((ITERS, group, OCTET, LAYER), f32),
            pltpu.VMEM((ITERS, group, OCTET, LAYER), f32),
            pltpu.VMEM((ITERS, OCTET, LAYER), f32),
            pltpu.VMEM((ITERS, depth, OCTET, LAYER), f32),
            pltpu.VMEM((ITERS, group, OCTET, LAYER), f32),
            pltpu.VMEM((ITERS, group, OCTET, LAYER), f32),
            dma((6,)), pltpu.SemaphoreType.REGULAR((depth,)), dma, dma, dma((depth,)), dma((depth,)), dma, dma,
            dma, dma, dma((ITERS,)), dma((ITERS,)),
            dma, dma, dma((ITERS,)), dma((ITERS,)),
            dma((ITERS, depth)), dma((ITERS, depth)), dma((ITERS,)), dma((ITERS,)),
        ],
        compiler_params=pltpu.CompilerParams(collective_id=1, has_side_effects=True),
        name="parareal",
    )(initial_state, inv_mass[None], element_scale[None], mode_rate, volume_block, face_blocks)
    return (half_sum + half_difference)[None], (half_sum - half_difference)[None]


def solution(mesh):
    slices = mesh.shape["tm"]
    group = (DOF // OCTET) * 2
    placed = (P(None, "space"), P("space"), P("space"), P("tm", None), P(), P())
    return jax.shard_map(
        functools.partial(per_device, slices // group, group),
        mesh=mesh,
        in_specs=placed,
        out_specs=(P("tm", None, "space"), P("tm", None, "space")),
        check_vma=False,
    )
```

```python
import functools

import jax
import jax.numpy as jnp
from jax import lax
from jax.experimental import pallas as pl
from jax.experimental.pallas import tpu as pltpu
from jax.sharding import PartitionSpec as P

DOF = 64
EY = 16
EZ = 8
FINE = 8
ITERS = 2
LAYER = EY * EZ
OCTET = 8
NEAR = 4
MESH = pl.DeviceIdType.MESH


def kernel(
    depth, group, shards,
    init_hbm, mass_hbm, scale_hbm, rate_hbm, volume_hbm, faces_hbm,
    sum_ref, difference_ref,
    init_ref, mass_ref, scale_ref, rate_ref, volume_ref, faces_ref,
    blocks, state, decay, coarse, guess_at, start, rounded, full, plane_guess, halo_src, halo, rows, row_src,
    rate_src, group_rates, tot_src, z_rates, pre_src, pre_dst,
    group_gain, z_gain, off_src, offs, sum_src, sums, run_src, run_dst, back_src, back,
    load, ready, rate_send, rate_recv, tot_send, tot_recv, pre_send, pre_recv, full_send, full_recv, halo_send, halo_recv,
    row_send, row_recv, off_send, off_recv, sum_send, sum_recv, run_send, run_recv, back_send, back_recv,
):
    cells = init_ref.shape[1]
    time = lax.axis_index("tm")
    mine = lax.axis_index("space")
    z = time // group
    j = lax.rem(time, group)

    def group_peer(q):
        return (z * group + q, mine)

    def z_peer(k):
        return (k * group + j, mine)

    def space_peer(p):
        return (time, p)

    def others(count, me, body):
        def step(d, carry):
            body(lax.rem(me + 1 + d, count))
            return carry

        lax.fori_loop(0, count - 1, step, 0)

    def nearest(body):
        lax.fori_loop(z + 1, jnp.minimum(z + NEAR, depth), lambda k, c: (body(k), c)[1], 0)

    def greet(peer):
        pl.semaphore_signal(barrier, inc=1, device_id=peer, device_id_type=MESH)

    def arrived(ref, sem):
        pltpu.make_async_copy(ref, ref, sem).wait()

    barrier = pltpu.get_barrier_semaphore()
    first_near = jnp.maximum(z - NEAR + 1, 0)
    others(group, j, lambda q: greet(group_peer(q)))
    others(shards, mine, lambda p: greet(space_peer(p)))
    lax.fori_loop(z + 1, jnp.minimum(z + NEAR + 1, depth), lambda k, c: (greet(z_peer(k)), c)[1], 0)

    loads = [
        pltpu.make_async_copy(src, dst, load.at[n])
        for n, (src, dst) in enumerate([
            (rate_hbm, rate_ref), (scale_hbm, scale_ref), (mass_hbm, mass_ref),
            (init_hbm, init_ref), (volume_hbm, volume_ref), (faces_hbm, faces_ref),
        ])
    ]
    for copy in loads:
        copy.start()

    zero_part = jnp.zeros((DOF, cells), jnp.bfloat16)
    rounded[0] = zero_part
    rounded[shards + 1] = zero_part
    sub = lax.broadcasted_iota(jnp.int32, (DOF, 128), 0)
    lane = lax.broadcasted_iota(jnp.int32, (DOF, 128), 1)
    sub_o = lax.broadcasted_iota(jnp.int32, (OCTET, 128), 0)
    lane_o = lax.broadcasted_iota(jnp.int32, (OCTET, 128), 1)
    first_mode = OCTET * j

    def column(values):
        return jnp.sum(jnp.where(sub == lane, values, 0.0), axis=1, keepdims=True)

    def octet_column(values):
        return jnp.sum(jnp.where(lane_o == sub_o + first_mode, values, 0.0), axis=1, keepdims=True)

    for copy in loads:
        copy.wait()
    row = jnp.concatenate([rate_ref[...], jnp.zeros((1, 128 - DOF), jnp.float32)], axis=1)
    rate_src[...] = row
    group_rates[pl.ds(j, 1)] = row[None]
    row_src[...] = jnp.concatenate(
        [mass_ref[...], scale_ref[...], jnp.zeros((6, cells), jnp.float32)], axis=0
    )
    rows[pl.ds(mine, 1)] = row_src[...][None]
    full[pl.ds(mine, 1)] = init_ref[...][None]
    blocks[:, :DOF] = volume_ref[...]
    for f in range(6):
        blocks[:, DOF * (f + 1) : DOF * (f + 2)] = faces_ref[f]
    own_scale = scale_ref[...]
    own_column = column(row)
    coarse[...] = jnp.exp(-(own_column * own_scale))

    pl.semaphore_wait(barrier, group + shards - 2 + jnp.minimum(z, NEAR))

    def rate_copy(q):
        return pltpu.make_async_remote_copy(
            src_ref=rate_src, dst_ref=group_rates.at[j], send_sem=rate_send, recv_sem=rate_recv,
            device_id=group_peer(q), device_id_type=MESH)

    def full_copy(p):
        return pltpu.make_async_remote_copy(
            src_ref=init_ref, dst_ref=full.at[mine], send_sem=full_send, recv_sem=full_recv,
            device_id=space_peer(p), device_id_type=MESH)

    def halo_copy(it, q, p):
        return pltpu.make_async_remote_copy(
            src_ref=halo_src.at[it, q], dst_ref=halo.at[it, mine, j], send_sem=halo_send.at[it],
            recv_sem=halo_recv.at[it], device_id=(z * group + q, p), device_id_type=MESH)

    def row_copy(p):
        return pltpu.make_async_remote_copy(
            src_ref=row_src, dst_ref=rows.at[mine], send_sem=row_send, recv_sem=row_recv,
            device_id=space_peer(p), device_id_type=MESH)

    others(group, j, lambda q: rate_copy(q).start())
    lax.fori_loop(
        0, jnp.minimum(z, NEAR),
        lambda k, c: (
            pl.semaphore_signal(ready.at[z], inc=1, device_id=z_peer(z - 1 - k), device_id_type=MESH), c)[1], 0)
    others(shards, mine, lambda p: row_copy(p).start())
    others(shards, mine, lambda p: full_copy(p).start())
    arrived(group_rates.at[pl.ds(0, group - 1)], rate_recv)
    total = jnp.zeros((1, 128), jnp.float32)
    before = jnp.zeros((1, 128), jnp.float32)
    for q in range(group):
        before = before + jnp.where(q < j, group_rates[q], 0.0)
        total = total + group_rates[q]
    tot_src[...] = total

    def tot_copy(k, slot):
        return pltpu.make_async_remote_copy(
            src_ref=tot_src, dst_ref=z_rates.at[slot], send_sem=tot_send.at[k], recv_sem=tot_recv.at[slot],
            device_id=z_peer(k), device_id_type=MESH)

    def tell(k, carry):
        pl.semaphore_wait(ready.at[k], 1)
        tot_copy(k, z).start()
        return carry

    lax.fori_loop(z + 1, jnp.minimum(z + 2, depth), tell, 0)

    for q in range(group):
        group_gain[q] = jnp.exp(-(octet_column(group_rates[q]) * own_scale))
    arrived(rows.at[pl.ds(0, shards - 1)], row_recv)
    for p in range(shards):
        decay[p] = jnp.exp(-(own_column * rows[p, 1:2, :]) / FINE)
    arrived(full.at[pl.ds(0, shards - 1)], full_recv)

    def pre_copy():
        return pltpu.make_async_remote_copy(
            src_ref=pre_src, dst_ref=pre_dst, send_sem=pre_send, recv_sem=pre_recv,
            device_id=z_peer(z + NEAR), device_id_type=MESH)

    lax.fori_loop(z + 2, jnp.minimum(z + NEAR, depth), tell, 0)

    pre_src[...] = jnp.zeros((1, 128), jnp.float32)

    @pl.when(z >= NEAR)
    def _():
        pre_copy().wait_recv()
        pre_src[...] = pre_dst[...]

    def add_total(k, carried):
        tot_copy(k, k).wait_recv()
        return carried + z_rates[k]

    ahead_of = lax.fori_loop(first_near, z, add_total, pre_src[...])
    pre_src[...] = ahead_of + total

    @pl.when(z + NEAR < depth)
    def _():
        pl.semaphore_wait(ready.at[z + NEAR], 1)
        pre_copy().start()

    passed = column(ahead_of + before)
    for p in range(shards):
        state[p] = jnp.exp(-(passed * rows[p, 1:2, :])) * full[p]
    guess = state[pl.ds(mine, 1)][0]
    guess_at[...] = guess
    start[...] = guess

    lane_t = lax.broadcasted_iota(jnp.int32, (2 * DOF, LAYER), 1)
    lane_z = lax.rem(lane_t, EZ)
    lower_of = lane_t - lane_z + lax.rem(lane_z + EZ - 1, EZ)
    upper_of = lane_t - lane_z + lax.rem(lane_z + 1, EZ)

    def fine_step(step, carry):
        for p in range(shards):
            rounded[p + 1] = state[p].astype(jnp.bfloat16)
        for p in range(shards):
            centre = rounded[p + 1]
            behind = jnp.concatenate([rounded[p, :, LAYER:], rounded[p + 1, :, :LAYER]], axis=1)
            ahead = jnp.concatenate([rounded[p + 1, :, LAYER:], rounded[p + 2, :, :LAYER]], axis=1)
            tall = jnp.concatenate([state[p, :, :LAYER], state[p, :, LAYER:]], axis=0)
            south = pltpu.roll(tall, EZ, 1)
            north = pltpu.roll(tall, LAYER - EZ, 1)
            lower = jnp.take_along_axis(tall, lower_of, axis=1, mode="promise_in_bounds")
            upper = jnp.take_along_axis(tall, upper_of, axis=1, mode="promise_in_bounds")

            def wide(value):
                value = value.astype(jnp.bfloat16)
                return jnp.concatenate([value[:DOF], value[DOF:]], axis=1)

            stacked = jnp.concatenate(
                [centre, behind, ahead, wide(south), wide(north), wide(lower), wide(upper)], axis=0
            )
            change = jnp.dot(blocks[...], stacked, preferred_element_type=jnp.float32)
            state[p] = decay[p] * state[p] + rows[p, 0:1, :] * change
        return carry

    offset = None
    for it in range(ITERS):
        lax.fori_loop(0, FINE, fine_step, 0, unroll=FINE)
        offset = state[pl.ds(mine, 1)][0] - coarse[...] * start[...]
        off_src[it] = offset.reshape(group, OCTET, cells)

        def off_copy(q):
            return pltpu.make_async_remote_copy(
                src_ref=off_src.at[it, q], dst_ref=offs.at[it, j], send_sem=off_send.at[it],
                recv_sem=off_recv.at[it], device_id=group_peer(q), device_id_type=MESH)

        others(group, j, lambda q: off_copy(q).start())
        offs[it, pl.ds(j, 1)] = off_src[it, pl.ds(j, 1)]
        if it == 0:
            def fill_gain(k, carry):
                z_gain[k] = jnp.exp(-(octet_column(z_rates[k]) * own_scale))
                return carry

            lax.fori_loop(first_near, z, fill_gain, 0)
            own_init = init_ref[pl.ds(pl.multiple_of(first_mode, OCTET), OCTET), :]
            since = ahead_of
            for q in range(group):
                plane_guess[q] = jnp.exp(-(octet_column(since) * own_scale)) * own_init
                since = since + group_rates[q]
        arrived(offs.at[it, pl.ds(0, group - 1)], off_recv.at[it])
        part = offs[it, 0]
        for q in range(1, group):
            part = group_gain[q] * part + offs[it, q]
        sum_src[it] = part

        def sum_copy(k, slot):
            return pltpu.make_async_remote_copy(
                src_ref=sum_src.at[it], dst_ref=sums.at[it, slot], send_sem=sum_send.at[it, k],
                recv_sem=sum_recv.at[it, slot], device_id=z_peer(k), device_id_type=MESH)

        nearest(lambda k: sum_copy(k, z).start())

        def run_copy():
            return pltpu.make_async_remote_copy(
                src_ref=run_src.at[it], dst_ref=run_dst.at[it], send_sem=run_send.at[it],
                recv_sem=run_recv.at[it], device_id=z_peer(z + NEAR), device_id_type=MESH)

        run_src[it] = jnp.zeros((OCTET, cells), jnp.float32)

        @pl.when(z >= NEAR)
        def _():
            run_copy().wait_recv()
            run_src[it] = run_dst[it]

        def add_sum(k, carried):
            sum_copy(k, k).wait_recv()
            return z_gain[k] * carried + sums[it, k]

        carried = lax.fori_loop(first_near, z, add_sum, run_src[it])
        for q in range(group):
            back_src[it, q] = carried
            carried = group_gain[q] * carried + offs[it, q]
        run_src[it] = carried

        @pl.when(z + NEAR < depth)
        def _():
            run_copy().start()

        def back_copy(q):
            return pltpu.make_async_remote_copy(
                src_ref=back_src.at[it, q], dst_ref=back.at[it, j], send_sem=back_send.at[it],
                recv_sem=back_recv.at[it], device_id=group_peer(q), device_id_type=MESH)

        others(group, j, lambda q: back_copy(q).start())
        if it + 1 < ITERS:
            for q in range(group):
                piece = plane_guess[q] + back_src[it, q]
                piece = jnp.concatenate([piece[:, n * LAYER : (n + 1) * LAYER] for n in range(2)], axis=0)
                halo_src[it, q] = piece.astype(jnp.bfloat16)

            def fan(p):
                others(group, j, lambda q: halo_copy(it, q, p).start())
                halo_copy(it, j, p).start()

            others(shards, mine, fan)
        back[it, pl.ds(j, 1)] = back_src[it, pl.ds(j, 1)]
        arrived(back.at[it, pl.ds(0, group - 1)], back_recv.at[it])
        correction = back[it].reshape(DOF, cells)
        following = guess_at[...] + correction
        if it + 1 < ITERS:
            start[...] = following
            arrived(halo.at[it, pl.ds(0, shards - 1)], halo_recv.at[it])
            for p in range(shards):
                for q in range(group):
                    piece = halo[it, p, q].astype(jnp.float32)
                    state[p, q * OCTET : (q + 1) * OCTET, :] = jnp.concatenate([piece[:OCTET], piece[OCTET:]], axis=1)
            state[pl.ds(mine, 1)] = following[None]
        else:
            end = 0.5 * (coarse[...] * following + offset)
            sum_ref[...] = end + 0.5 * guess_at[...]
            difference_ref[...] = end - 0.5 * guess_at[...]

    def left(ref, sem):
        pltpu.make_async_copy(ref, ref, sem).wait()

    left(group_rates.at[pl.ds(0, group - 1)], rate_send)
    left(rows.at[pl.ds(0, shards - 1)], row_send)
    left(full.at[pl.ds(0, shards - 1)], full_send)
    nearest(lambda k: tot_copy(k, z).wait_send())

    @pl.when(z + NEAR < depth)
    def _():
        pre_copy().wait_send()

    for it in range(ITERS):
        left(off_src.at[it, pl.ds(0, group - 1)], off_send.at[it])
        left(back_src.at[it, pl.ds(0, group - 1)], back_send.at[it])
        if it + 1 < ITERS:
            left(halo.at[it, pl.ds(0, shards - 1)], halo_send.at[it])

        def summed(k):
            pltpu.make_async_copy(sum_src.at[it], sum_src.at[it], sum_send.at[it, k]).wait()

        nearest(summed)

        @pl.when(z + NEAR < depth)
        def _():
            pltpu.make_async_copy(run_src.at[it], run_src.at[it], run_send.at[it]).wait()


def per_device(depth, group, initial_state, inv_mass, element_scale, mode_rate, volume_block, face_blocks):
    shards = lax.axis_size("space")
    cells = initial_state.shape[1]
    f32, bf16 = jnp.float32, jnp.bfloat16
    vmem = pl.BlockSpec(memory_space=pltpu.VMEM)
    hbm = pl.BlockSpec(memory_space=pltpu.HBM)
    dma = pltpu.SemaphoreType.DMA
    half_sum, half_difference = pl.pallas_call(
        functools.partial(kernel, depth, group, shards),
        out_shape=[pltpu.VMEM((DOF, cells), f32)] * 2,
        in_specs=[hbm] * 6,
        out_specs=[vmem] * 2,
        scratch_shapes=[
            pltpu.VMEM((DOF, cells), f32),
            pltpu.VMEM((1, cells), f32),
            pltpu.VMEM((1, cells), f32),
            pltpu.VMEM((1, DOF), f32),
            pltpu.VMEM((DOF, DOF), bf16),
            pltpu.VMEM((6, DOF, DOF), bf16),
            pltpu.VMEM((DOF, 7 * DOF), bf16),
            pltpu.VMEM((shards, DOF, cells), f32),
            pltpu.VMEM((shards, DOF, cells), f32),
            pltpu.VMEM((DOF, cells), f32),
            pltpu.VMEM((DOF, cells), f32),
            pltpu.VMEM((DOF, cells), f32),
            pltpu.VMEM((shards + 2, DOF, cells), bf16),
            pltpu.VMEM((shards, DOF, cells), f32),
            pltpu.VMEM((group, OCTET, cells), f32),
            pltpu.VMEM((ITERS - 1, group, 2 * OCTET, LAYER), bf16),
            pltpu.VMEM((ITERS - 1, shards, group, 2 * OCTET, LAYER), bf16),
            pltpu.VMEM((shards, 8, cells), f32),
            pltpu.VMEM((8, cells), f32),
            pltpu.VMEM((1, 128), f32),
            pltpu.VMEM((group, 1, 128), f32),
            pltpu.VMEM((1, 128), f32),
            pltpu.VMEM((depth, 1, 128), f32),
            pltpu.VMEM((1, 128), f32),
            pltpu.VMEM((1, 128), f32),
            pltpu.VMEM((group, OCTET, cells), f32),
            pltpu.VMEM((depth, OCTET, cells), f32),
            pltpu.VMEM((ITERS, group, OCTET, cells), f32),
            pltpu.VMEM((ITERS, group, OCTET, cells), f32),
            pltpu.VMEM((ITERS, OCTET, cells), f32),
            pltpu.VMEM((ITERS, depth, OCTET, cells), f32),
            pltpu.VMEM((ITERS, OCTET, cells), f32),
            pltpu.VMEM((ITERS, OCTET, cells), f32),
            pltpu.VMEM((ITERS, group, OCTET, cells), f32),
            pltpu.VMEM((ITERS, group, OCTET, cells), f32),
            dma((6,)), pltpu.SemaphoreType.REGULAR((depth,)), dma, dma, dma((depth,)), dma((depth,)), dma, dma,
            dma, dma, dma((ITERS,)), dma((ITERS,)),
            dma, dma, dma((ITERS,)), dma((ITERS,)),
            dma((ITERS, depth)), dma((ITERS, depth)), dma((ITERS,)), dma((ITERS,)), dma((ITERS,)), dma((ITERS,)),
        ],
        compiler_params=pltpu.CompilerParams(collective_id=1, has_side_effects=True),
        name="parareal",
    )(initial_state, inv_mass[None], element_scale[None], mode_rate, volume_block, face_blocks)
    return (half_sum + half_difference)[None], (half_sum - half_difference)[None]


def solution(mesh):
    slices = mesh.shape["tm"]
    group = DOF // OCTET
    placed = (P(None, "space"), P("space"), P("space"), P("tm", None), P(), P())
    return jax.shard_map(
        functools.partial(per_device, slices // group, group),
        mesh=mesh,
        in_specs=placed,
        out_specs=(P("tm", None, "space"), P("tm", None, "space")),
        check_vma=False,
    )
```

```python
import functools

import jax
import jax.numpy as jnp
from jax import lax
from jax.experimental import pallas as pl
from jax.experimental.pallas import tpu as pltpu
from jax.sharding import PartitionSpec as P

DOF = 64
EY = 16
EZ = 8
FINE = 8
ITERS = 2
LAYER = EY * EZ
OCTET = 8
NEAR = 4
MESH = pl.DeviceIdType.MESH


def kernel(
    depth, group, shards,
    init_hbm, mass_hbm, scale_hbm, rate_hbm, volume_hbm, faces_hbm,
    sum_ref, difference_ref,
    init_ref, mass_ref, scale_ref, rate_ref, volume_ref, faces_ref,
    blocks, state, decay, coarse, guess_at, start, rounded, full, plane_guess, halo_src, halo, rows, row_src,
    rate_src, group_rates, tot_src, z_rates, pre_src, pre_dst,
    group_gain, z_gain, off_src, offs, sum_src, sums, run_src, run_dst, back_src, back,
    load, ready, rate_send, rate_recv, tot_send, tot_recv, pre_send, pre_recv, full_send, full_recv, halo_send, halo_recv,
    row_send, row_recv, off_send, off_recv, sum_send, sum_recv, run_send, run_recv, back_send, back_recv,
):
    cells = init_ref.shape[1]
    time = lax.axis_index("tm")
    mine = lax.axis_index("space")
    z = time // group
    j = lax.rem(time, group)

    def group_peer(q):
        return (z * group + q, mine)

    def z_peer(k):
        return (k * group + j, mine)

    def space_peer(p):
        return (time, p)

    def others(count, me, body):
        def step(d, carry):
            body(lax.rem(me + 1 + d, count))
            return carry

        lax.fori_loop(0, count - 1, step, 0, unroll=True)

    def nearest(body):
        lax.fori_loop(z + 1, jnp.minimum(z + NEAR, depth), lambda k, c: (body(k), c)[1], 0)

    def greet(peer):
        pl.semaphore_signal(barrier, inc=1, device_id=peer, device_id_type=MESH)

    def arrived(ref, sem):
        pltpu.make_async_copy(ref, ref, sem).wait()

    barrier = pltpu.get_barrier_semaphore()
    first_near = jnp.maximum(z - NEAR + 1, 0)
    others(group, j, lambda q: greet(group_peer(q)))
    others(shards, mine, lambda p: greet(space_peer(p)))
    lax.fori_loop(z + 1, jnp.minimum(z + NEAR + 1, depth), lambda k, c: (greet(z_peer(k)), c)[1], 0)

    loads = [
        pltpu.make_async_copy(src, dst, load.at[n])
        for n, (src, dst) in enumerate([
            (rate_hbm, rate_ref), (scale_hbm, scale_ref), (mass_hbm, mass_ref),
            (init_hbm, init_ref), (volume_hbm, volume_ref), (faces_hbm, faces_ref),
        ])
    ]
    for copy in loads:
        copy.start()

    zero_part = jnp.zeros((DOF, cells), jnp.bfloat16)
    rounded[0] = zero_part
    rounded[shards + 1] = zero_part
    sub = lax.broadcasted_iota(jnp.int32, (DOF, 128), 0)
    lane = lax.broadcasted_iota(jnp.int32, (DOF, 128), 1)
    sub_o = lax.broadcasted_iota(jnp.int32, (OCTET, 128), 0)
    lane_o = lax.broadcasted_iota(jnp.int32, (OCTET, 128), 1)
    first_mode = OCTET * j

    def column(values):
        return jnp.sum(jnp.where(sub == lane, values, 0.0), axis=1, keepdims=True)

    def octet_column(values):
        return jnp.sum(jnp.where(lane_o == sub_o + first_mode, values, 0.0), axis=1, keepdims=True)

    for copy in loads:
        copy.wait()
    row = jnp.concatenate([rate_ref[...], jnp.zeros((1, 128 - DOF), jnp.float32)], axis=1)
    rate_src[...] = row
    group_rates[pl.ds(j, 1)] = row[None]
    row_src[...] = jnp.concatenate(
        [mass_ref[...], scale_ref[...], jnp.zeros((6, cells), jnp.float32)], axis=0
    )
    rows[pl.ds(mine, 1)] = row_src[...][None]
    full[pl.ds(mine, 1)] = init_ref[...][None]
    blocks[:, :DOF] = volume_ref[...]
    for f in range(6):
        blocks[:, DOF * (f + 1) : DOF * (f + 2)] = faces_ref[f]
    own_scale = scale_ref[...]
    own_column = column(row)
    coarse[...] = jnp.exp(-(own_column * own_scale))

    pl.semaphore_wait(barrier, group + shards - 2 + jnp.minimum(z, NEAR))

    def rate_copy(q):
        return pltpu.make_async_remote_copy(
            src_ref=rate_src, dst_ref=group_rates.at[j], send_sem=rate_send, recv_sem=rate_recv,
            device_id=group_peer(q), device_id_type=MESH)

    def full_copy(p):
        return pltpu.make_async_remote_copy(
            src_ref=init_ref, dst_ref=full.at[mine], send_sem=full_send, recv_sem=full_recv,
            device_id=space_peer(p), device_id_type=MESH)

    def halo_copy(it, q, p):
        return pltpu.make_async_remote_copy(
            src_ref=halo_src.at[it, q], dst_ref=halo.at[it, mine, j], send_sem=halo_send.at[it],
            recv_sem=halo_recv.at[it], device_id=(z * group + q, p), device_id_type=MESH)

    def row_copy(p):
        return pltpu.make_async_remote_copy(
            src_ref=row_src, dst_ref=rows.at[mine], send_sem=row_send, recv_sem=row_recv,
            device_id=space_peer(p), device_id_type=MESH)

    others(group, j, lambda q: rate_copy(q).start())
    lax.fori_loop(
        0, jnp.minimum(z, NEAR),
        lambda k, c: (
            pl.semaphore_signal(ready.at[z], inc=1, device_id=z_peer(z - 1 - k), device_id_type=MESH), c)[1], 0)
    others(shards, mine, lambda p: row_copy(p).start())
    others(shards, mine, lambda p: full_copy(p).start())
    arrived(group_rates.at[pl.ds(0, group - 1)], rate_recv)
    total = jnp.zeros((1, 128), jnp.float32)
    before = jnp.zeros((1, 128), jnp.float32)
    for q in range(group):
        before = before + jnp.where(q < j, group_rates[q], 0.0)
        total = total + group_rates[q]
    tot_src[...] = total

    def tot_copy(k, slot):
        return pltpu.make_async_remote_copy(
            src_ref=tot_src, dst_ref=z_rates.at[slot], send_sem=tot_send.at[k], recv_sem=tot_recv.at[slot],
            device_id=z_peer(k), device_id_type=MESH)

    def tell(k, carry):
        pl.semaphore_wait(ready.at[k], 1)
        tot_copy(k, z).start()
        return carry

    lax.fori_loop(z + 1, jnp.minimum(z + 2, depth), tell, 0)

    for q in range(group):
        group_gain[q] = jnp.exp(-(octet_column(group_rates[q]) * own_scale))
    arrived(rows.at[pl.ds(0, shards - 1)], row_recv)
    for p in range(shards):
        decay[p] = jnp.exp(-(own_column * rows[p, 1:2, :]) / FINE)
    arrived(full.at[pl.ds(0, shards - 1)], full_recv)

    def pre_copy():
        return pltpu.make_async_remote_copy(
            src_ref=pre_src, dst_ref=pre_dst, send_sem=pre_send, recv_sem=pre_recv,
            device_id=z_peer(z + NEAR), device_id_type=MESH)

    lax.fori_loop(z + 2, jnp.minimum(z + NEAR, depth), tell, 0)

    pre_src[...] = jnp.zeros((1, 128), jnp.float32)

    @pl.when(z >= NEAR)
    def _():
        pre_copy().wait_recv()
        pre_src[...] = pre_dst[...]

    def add_total(k, carried):
        tot_copy(k, k).wait_recv()
        return carried + z_rates[k]

    ahead_of = lax.fori_loop(first_near, z, add_total, pre_src[...])
    pre_src[...] = ahead_of + total

    @pl.when(z + NEAR < depth)
    def _():
        pl.semaphore_wait(ready.at[z + NEAR], 1)
        pre_copy().start()

    passed = column(ahead_of + before)
    for p in range(shards):
        state[p] = jnp.exp(-(passed * rows[p, 1:2, :])) * full[p]
    guess = state[pl.ds(mine, 1)][0]
    guess_at[...] = guess
    start[...] = guess

    lane_t = lax.broadcasted_iota(jnp.int32, (2 * DOF, LAYER), 1)
    lane_z = lax.rem(lane_t, EZ)
    lower_of = lane_t - lane_z + lax.rem(lane_z + EZ - 1, EZ)
    upper_of = lane_t - lane_z + lax.rem(lane_z + 1, EZ)

    def fine_step(step, carry):
        for p in range(shards):
            rounded[p + 1] = state[p].astype(jnp.bfloat16)
        for p in range(shards):
            centre = rounded[p + 1]
            behind = jnp.concatenate([rounded[p, :, LAYER:], rounded[p + 1, :, :LAYER]], axis=1)
            ahead = jnp.concatenate([rounded[p + 1, :, LAYER:], rounded[p + 2, :, :LAYER]], axis=1)
            tall = jnp.concatenate([state[p, :, :LAYER], state[p, :, LAYER:]], axis=0)
            south = pltpu.roll(tall, EZ, 1)
            north = pltpu.roll(tall, LAYER - EZ, 1)
            lower = jnp.take_along_axis(tall, lower_of, axis=1, mode="promise_in_bounds")
            upper = jnp.take_along_axis(tall, upper_of, axis=1, mode="promise_in_bounds")

            def wide(value):
                value = value.astype(jnp.bfloat16)
                return jnp.concatenate([value[:DOF], value[DOF:]], axis=1)

            stacked = jnp.concatenate(
                [centre, behind, ahead, wide(south), wide(north), wide(lower), wide(upper)], axis=0
            )
            change = jnp.dot(blocks[...], stacked, preferred_element_type=jnp.float32)
            state[p] = decay[p] * state[p] + rows[p, 0:1, :] * change
        return carry

    def leave():
        def left(ref, sem):
            pltpu.make_async_copy(ref, ref, sem).wait()

        left(group_rates.at[pl.ds(0, group - 1)], rate_send)
        left(rows.at[pl.ds(0, shards - 1)], row_send)
        left(full.at[pl.ds(0, shards - 1)], full_send)
        nearest(lambda k: tot_copy(k, z).wait_send())

        @pl.when(z + NEAR < depth)
        def _():
            pre_copy().wait_send()

        for it in range(ITERS):
            left(off_src.at[it, pl.ds(0, group - 1)], off_send.at[it])
            if it + 1 < ITERS:
                left(back_src.at[it, pl.ds(0, group - 1)], back_send.at[it])
            if it + 1 < ITERS:
                left(halo.at[it, pl.ds(0, shards - 1)], halo_send.at[it])

            def summed(k):
                pltpu.make_async_copy(sum_src.at[it], sum_src.at[it], sum_send.at[it, k]).wait()

            nearest(summed)

            @pl.when(z + NEAR < depth)
            def _():
                pltpu.make_async_copy(run_src.at[it], run_src.at[it], run_send.at[it]).wait()

    offset = None
    for it in range(ITERS):
        lax.fori_loop(0, FINE, fine_step, 0, unroll=FINE)
        offset = state[pl.ds(mine, 1)][0] - coarse[...] * start[...]
        off_src[it] = offset.reshape(group, OCTET, cells)

        def off_copy(q):
            return pltpu.make_async_remote_copy(
                src_ref=off_src.at[it, q], dst_ref=offs.at[it, j], send_sem=off_send.at[it],
                recv_sem=off_recv.at[it], device_id=group_peer(q), device_id_type=MESH)

        others(group, j, lambda q: off_copy(q).start())
        offs[it, pl.ds(j, 1)] = off_src[it, pl.ds(j, 1)]
        if it == 0:
            def fill_gain(k, carry):
                z_gain[k] = jnp.exp(-(octet_column(z_rates[k]) * own_scale))
                return carry

            lax.fori_loop(first_near, z, fill_gain, 0)
            own_init = init_ref[pl.ds(pl.multiple_of(first_mode, OCTET), OCTET), :]
            since = ahead_of
            for q in range(group):
                plane_guess[q] = jnp.exp(-(octet_column(since) * own_scale)) * own_init
                since = since + group_rates[q]
        arrived(offs.at[it, pl.ds(0, group - 1)], off_recv.at[it])
        part = offs[it, 0]
        for q in range(1, group):
            part = group_gain[q] * part + offs[it, q]
        sum_src[it] = part

        def sum_copy(k, slot):
            return pltpu.make_async_remote_copy(
                src_ref=sum_src.at[it], dst_ref=sums.at[it, slot], send_sem=sum_send.at[it, k],
                recv_sem=sum_recv.at[it, slot], device_id=z_peer(k), device_id_type=MESH)

        nearest(lambda k: sum_copy(k, z).start())

        def run_copy():
            return pltpu.make_async_remote_copy(
                src_ref=run_src.at[it], dst_ref=run_dst.at[it], send_sem=run_send.at[it],
                recv_sem=run_recv.at[it], device_id=z_peer(z + NEAR), device_id_type=MESH)

        run_src[it] = jnp.zeros((OCTET, cells), jnp.float32)

        @pl.when(z >= NEAR)
        def _():
            run_copy().wait_recv()
            run_src[it] = run_dst[it]

        def add_sum(k, carried):
            sum_copy(k, k).wait_recv()
            return z_gain[k] * carried + sums[it, k]

        carried = lax.fori_loop(first_near, z, add_sum, run_src[it])
        for q in range(group):
            back_src[it, q] = carried
            carried = group_gain[q] * carried + offs[it, q]
        run_src[it] = carried

        @pl.when(z + NEAR < depth)
        def _():
            run_copy().start()

        def back_copy(q):
            return pltpu.make_async_remote_copy(
                src_ref=back_src.at[it, q], dst_ref=back.at[it, j], send_sem=back_send.at[it],
                recv_sem=back_recv.at[it], device_id=group_peer(q), device_id_type=MESH)

        if it + 1 < ITERS:
            for q in range(group):
                piece = plane_guess[q] + back_src[it, q]
                piece = jnp.concatenate([piece[:, n * LAYER : (n + 1) * LAYER] for n in range(2)], axis=0)
                halo_src[it, q] = piece.astype(jnp.bfloat16)

            def fan(p):
                others(group, j, lambda q: halo_copy(it, q, p).start())
                halo_copy(it, j, p).start()

            others(shards, mine, fan)

        others(group, j, lambda q: back_copy(q).start())
        back[it, pl.ds(j, 1)] = back_src[it, pl.ds(j, 1)]
        if it + 1 == ITERS:
            leave()
        arrived(back.at[it, pl.ds(0, group - 1)], back_recv.at[it])
        correction = back[it].reshape(DOF, cells)
        following = guess_at[...] + correction
        if it + 1 < ITERS:
            start[...] = following
            arrived(halo.at[it, pl.ds(0, shards - 1)], halo_recv.at[it])
            for p in range(shards):
                for q in range(group):
                    piece = halo[it, p, q].astype(jnp.float32)
                    state[p, q * OCTET : (q + 1) * OCTET, :] = jnp.concatenate([piece[:OCTET], piece[OCTET:]], axis=1)
            state[pl.ds(mine, 1)] = following[None]
        else:
            end = 0.5 * (coarse[...] * following + offset)
            sum_ref[...] = end + 0.5 * guess_at[...]
            difference_ref[...] = end - 0.5 * guess_at[...]
            arrived(back_src.at[it, pl.ds(0, group - 1)], back_send.at[it])


def per_device(depth, group, initial_state, inv_mass, element_scale, mode_rate, volume_block, face_blocks):
    shards = lax.axis_size("space")
    cells = initial_state.shape[1]
    f32, bf16 = jnp.float32, jnp.bfloat16
    vmem = pl.BlockSpec(memory_space=pltpu.VMEM)
    hbm = pl.BlockSpec(memory_space=pltpu.HBM)
    dma = pltpu.SemaphoreType.DMA
    half_sum, half_difference = pl.pallas_call(
        functools.partial(kernel, depth, group, shards),
        out_shape=[pltpu.VMEM((DOF, cells), f32)] * 2,
        in_specs=[hbm] * 6,
        out_specs=[vmem] * 2,
        scratch_shapes=[
            pltpu.VMEM((DOF, cells), f32),
            pltpu.VMEM((1, cells), f32),
            pltpu.VMEM((1, cells), f32),
            pltpu.VMEM((1, DOF), f32),
            pltpu.VMEM((DOF, DOF), bf16),
            pltpu.VMEM((6, DOF, DOF), bf16),
            pltpu.VMEM((DOF, 7 * DOF), bf16),
            pltpu.VMEM((shards, DOF, cells), f32),
            pltpu.VMEM((shards, DOF, cells), f32),
            pltpu.VMEM((DOF, cells), f32),
            pltpu.VMEM((DOF, cells), f32),
            pltpu.VMEM((DOF, cells), f32),
            pltpu.VMEM((shards + 2, DOF, cells), bf16),
            pltpu.VMEM((shards, DOF, cells), f32),
            pltpu.VMEM((group, OCTET, cells), f32),
            pltpu.VMEM((ITERS - 1, group, 2 * OCTET, LAYER), bf16),
            pltpu.VMEM((ITERS - 1, shards, group, 2 * OCTET, LAYER), bf16),
            pltpu.VMEM((shards, 8, cells), f32),
            pltpu.VMEM((8, cells), f32),
            pltpu.VMEM((1, 128), f32),
            pltpu.VMEM((group, 1, 128), f32),
            pltpu.VMEM((1, 128), f32),
            pltpu.VMEM((depth, 1, 128), f32),
            pltpu.VMEM((1, 128), f32),
            pltpu.VMEM((1, 128), f32),
            pltpu.VMEM((group, OCTET, cells), f32),
            pltpu.VMEM((depth, OCTET, cells), f32),
            pltpu.VMEM((ITERS, group, OCTET, cells), f32),
            pltpu.VMEM((ITERS, group, OCTET, cells), f32),
            pltpu.VMEM((ITERS, OCTET, cells), f32),
            pltpu.VMEM((ITERS, depth, OCTET, cells), f32),
            pltpu.VMEM((ITERS, OCTET, cells), f32),
            pltpu.VMEM((ITERS, OCTET, cells), f32),
            pltpu.VMEM((ITERS, group, OCTET, cells), f32),
            pltpu.VMEM((ITERS, group, OCTET, cells), f32),
            dma((6,)), pltpu.SemaphoreType.REGULAR((depth,)), dma, dma, dma((depth,)), dma((depth,)), dma, dma,
            dma, dma, dma((ITERS,)), dma((ITERS,)),
            dma, dma, dma((ITERS,)), dma((ITERS,)),
            dma((ITERS, depth)), dma((ITERS, depth)), dma((ITERS,)), dma((ITERS,)), dma((ITERS,)), dma((ITERS,)),
        ],
        compiler_params=pltpu.CompilerParams(collective_id=1, has_side_effects=True),
        name="parareal",
    )(initial_state, inv_mass[None], element_scale[None], mode_rate, volume_block, face_blocks)
    return (half_sum + half_difference)[None], (half_sum - half_difference)[None]


def solution(mesh):
    slices = mesh.shape["tm"]
    group = DOF // OCTET
    placed = (P(None, "space"), P("space"), P("space"), P("tm", None), P(), P())
    return jax.shard_map(
        functools.partial(per_device, slices // group, group),
        mesh=mesh,
        in_specs=placed,
        out_specs=(P("tm", None, "space"), P("tm", None, "space")),
        check_vma=False,
    )
```

```python
import functools

import jax
import jax.numpy as jnp
from jax import lax
from jax.experimental import pallas as pl
from jax.experimental.pallas import tpu as pltpu
from jax.sharding import PartitionSpec as P

DOF = 64
EY = 16
EZ = 8
FINE = 8
ITERS = 2
LAYER = EY * EZ
OCTET = 8
NEAR = 4
MESH = pl.DeviceIdType.MESH


def kernel(
    depth, group, shards,
    init_hbm, mass_hbm, scale_hbm, rate_hbm, volume_hbm, faces_hbm,
    sum_ref, difference_ref,
    init_ref, mass_ref, scale_ref, rate_ref, volume_ref, faces_ref,
    blocks, state, decay, mass, coarse, guess_at, start, full, plane_guess, halo_src, halo, rows, row_src,
    rate_src, group_rates, tot_src, z_rates, pre_src, pre_dst,
    group_gain, z_gain, off_src, offs, sum_src, sums, run_src, run_dst, back_src, back,
    load, ready, rate_send, rate_recv, tot_send, tot_recv, pre_send, pre_recv, full_send, full_recv, halo_send, halo_recv,
    row_send, row_recv, off_send, off_recv, sum_send, sum_recv, run_send, run_recv, back_send, back_recv,
):
    cells = init_ref.shape[1]
    time = lax.axis_index("tm")
    mine = lax.axis_index("space")
    z = time // group
    j = lax.rem(time, group)

    def group_peer(q):
        return (z * group + q, mine)

    def z_peer(k):
        return (k * group + j, mine)

    def space_peer(p):
        return (time, p)

    def others(count, me, body):
        def step(d, carry):
            body(lax.rem(me + 1 + d, count))
            return carry

        lax.fori_loop(0, count - 1, step, 0, unroll=True)

    def nearest(body):
        lax.fori_loop(z + 1, jnp.minimum(z + NEAR, depth), lambda k, c: (body(k), c)[1], 0)

    def greet(peer):
        pl.semaphore_signal(barrier, inc=1, device_id=peer, device_id_type=MESH)

    def arrived(ref, sem):
        pltpu.make_async_copy(ref, ref, sem).wait()

    barrier = pltpu.get_barrier_semaphore()
    first_near = jnp.maximum(z - NEAR + 1, 0)
    others(group, j, lambda q: greet(group_peer(q)))
    others(shards, mine, lambda p: greet(space_peer(p)))
    lax.fori_loop(z + 1, jnp.minimum(z + NEAR + 1, depth), lambda k, c: (greet(z_peer(k)), c)[1], 0)

    loads = [
        pltpu.make_async_copy(src, dst, load.at[n])
        for n, (src, dst) in enumerate([
            (rate_hbm, rate_ref), (scale_hbm, scale_ref), (mass_hbm, mass_ref),
            (init_hbm, init_ref), (volume_hbm, volume_ref), (faces_hbm, faces_ref),
        ])
    ]
    for copy in loads:
        copy.start()

    sub = lax.broadcasted_iota(jnp.int32, (DOF, 128), 0)
    lane = lax.broadcasted_iota(jnp.int32, (DOF, 128), 1)
    sub_o = lax.broadcasted_iota(jnp.int32, (OCTET, 128), 0)
    lane_o = lax.broadcasted_iota(jnp.int32, (OCTET, 128), 1)
    first_mode = OCTET * j

    def column(values):
        return jnp.sum(jnp.where(sub == lane, values, 0.0), axis=1, keepdims=True)

    def octet_column(values):
        return jnp.sum(jnp.where(lane_o == sub_o + first_mode, values, 0.0), axis=1, keepdims=True)

    for copy in loads:
        copy.wait()
    row = jnp.concatenate([rate_ref[...], jnp.zeros((1, 128 - DOF), jnp.float32)], axis=1)
    rate_src[...] = row
    group_rates[pl.ds(j, 1)] = row[None]
    row_src[...] = jnp.concatenate(
        [mass_ref[...], scale_ref[...], jnp.zeros((6, cells), jnp.float32)], axis=0
    )
    rows[pl.ds(mine, 1)] = row_src[...][None]
    full[pl.ds(mine, 1)] = init_ref[...][None]
    turned = [volume_ref[...]] + [faces_ref[f] for f in range(6)]
    turned = [block.astype(jnp.float32).T.astype(jnp.bfloat16) for block in turned]
    none = jnp.zeros((DOF, DOF), jnp.bfloat16)
    grid = [[turned[0], turned[1]], [turned[2], turned[0]], [none, turned[2]], [turned[1], none]]
    for f in range(3, 7):
        grid += [[turned[f], none], [none, turned[f]]]
    for n, (left_block, right_block) in enumerate(grid):
        blocks[DOF * n : DOF * (n + 1), :DOF] = left_block
        blocks[DOF * n : DOF * (n + 1), DOF:] = right_block

    def tall(value):
        return jnp.concatenate([value[:, :LAYER], value[:, LAYER:]], axis=0).T

    def flat(value):
        value = value.T
        return jnp.concatenate([value[:DOF], value[DOF:]], axis=1)

    own_scale = scale_ref[...]
    own_column = column(row)
    coarse[...] = jnp.exp(-(own_column * own_scale))

    pl.semaphore_wait(barrier, group + shards - 2 + jnp.minimum(z, NEAR))

    def rate_copy(q):
        return pltpu.make_async_remote_copy(
            src_ref=rate_src, dst_ref=group_rates.at[j], send_sem=rate_send, recv_sem=rate_recv,
            device_id=group_peer(q), device_id_type=MESH)

    def full_copy(p):
        return pltpu.make_async_remote_copy(
            src_ref=init_ref, dst_ref=full.at[mine], send_sem=full_send, recv_sem=full_recv,
            device_id=space_peer(p), device_id_type=MESH)

    def halo_copy(it, q, p):
        return pltpu.make_async_remote_copy(
            src_ref=halo_src.at[it, q], dst_ref=halo.at[it, mine, j], send_sem=halo_send.at[it],
            recv_sem=halo_recv.at[it], device_id=(z * group + q, p), device_id_type=MESH)

    def row_copy(p):
        return pltpu.make_async_remote_copy(
            src_ref=row_src, dst_ref=rows.at[mine], send_sem=row_send, recv_sem=row_recv,
            device_id=space_peer(p), device_id_type=MESH)

    others(group, j, lambda q: rate_copy(q).start())
    lax.fori_loop(
        0, jnp.minimum(z, NEAR),
        lambda k, c: (
            pl.semaphore_signal(ready.at[z], inc=1, device_id=z_peer(z - 1 - k), device_id_type=MESH), c)[1], 0)
    others(shards, mine, lambda p: row_copy(p).start())
    others(shards, mine, lambda p: full_copy(p).start())
    arrived(group_rates.at[pl.ds(0, group - 1)], rate_recv)
    total = jnp.zeros((1, 128), jnp.float32)
    before = jnp.zeros((1, 128), jnp.float32)
    for q in range(group):
        before = before + jnp.where(q < j, group_rates[q], 0.0)
        total = total + group_rates[q]
    tot_src[...] = total

    def tot_copy(k, slot):
        return pltpu.make_async_remote_copy(
            src_ref=tot_src, dst_ref=z_rates.at[slot], send_sem=tot_send.at[k], recv_sem=tot_recv.at[slot],
            device_id=z_peer(k), device_id_type=MESH)

    def tell(k, carry):
        pl.semaphore_wait(ready.at[k], 1)
        tot_copy(k, z).start()
        return carry

    lax.fori_loop(z + 1, jnp.minimum(z + 2, depth), tell, 0)

    for q in range(group):
        group_gain[q] = jnp.exp(-(octet_column(group_rates[q]) * own_scale))
    arrived(rows.at[pl.ds(0, shards - 1)], row_recv)
    for p in range(shards):
        decay[p] = tall(jnp.exp(-(own_column * rows[p, 1:2, :]) / FINE))
        mass[p] = tall(jnp.broadcast_to(rows[p, 0:1, :], (DOF, cells)))
    arrived(full.at[pl.ds(0, shards - 1)], full_recv)

    def pre_copy():
        return pltpu.make_async_remote_copy(
            src_ref=pre_src, dst_ref=pre_dst, send_sem=pre_send, recv_sem=pre_recv,
            device_id=z_peer(z + NEAR), device_id_type=MESH)

    lax.fori_loop(z + 2, jnp.minimum(z + NEAR, depth), tell, 0)

    pre_src[...] = jnp.zeros((1, 128), jnp.float32)

    @pl.when(z >= NEAR)
    def _():
        pre_copy().wait_recv()
        pre_src[...] = pre_dst[...]

    def add_total(k, carried):
        tot_copy(k, k).wait_recv()
        return carried + z_rates[k]

    ahead_of = lax.fori_loop(first_near, z, add_total, pre_src[...])
    pre_src[...] = ahead_of + total

    @pl.when(z + NEAR < depth)
    def _():
        pl.semaphore_wait(ready.at[z + NEAR], 1)
        pre_copy().start()

    passed = column(ahead_of + before)
    for p in range(shards):
        state[p] = tall(jnp.exp(-(passed * rows[p, 1:2, :])) * full[p])
    guess = jnp.exp(-(passed * own_scale)) * init_ref[...]
    guess_at[...] = guess
    start[...] = guess

    low = lax.broadcasted_iota(jnp.int32, (LAYER, 2 * DOF), 1) < DOF

    def turn(value, by):
        return pltpu.roll(value.reshape(EY, EZ, 2 * DOF), by, 1).reshape(LAYER, 2 * DOF)

    def fine_step(step, carry):
        old = [state[p] for p in range(shards)]
        edge = jnp.zeros((LAYER, 2 * DOF), jnp.float32)
        for p in range(shards):
            value = old[p]
            beside = jnp.where(low, old[p + 1] if p + 1 < shards else edge, old[p - 1] if p else edge)
            parts = [
                value, beside, pltpu.roll(value, EZ, 0), pltpu.roll(value, LAYER - EZ, 0),
                turn(value, 1), turn(value, EZ - 1),
            ]
            stacked = jnp.concatenate([part.astype(jnp.bfloat16) for part in parts], axis=1)
            change = jnp.dot(stacked, blocks[...], preferred_element_type=jnp.float32)
            state[p] = decay[p] * value + mass[p] * change
        return carry

    def leave():
        def left(ref, sem):
            pltpu.make_async_copy(ref, ref, sem).wait()

        left(group_rates.at[pl.ds(0, group - 1)], rate_send)
        left(rows.at[pl.ds(0, shards - 1)], row_send)
        left(full.at[pl.ds(0, shards - 1)], full_send)
        nearest(lambda k: tot_copy(k, z).wait_send())

        @pl.when(z + NEAR < depth)
        def _():
            pre_copy().wait_send()

        for it in range(ITERS):
            left(off_src.at[it, pl.ds(0, group - 1)], off_send.at[it])
            if it + 1 < ITERS:
                left(back_src.at[it, pl.ds(0, group - 1)], back_send.at[it])
            if it + 1 < ITERS:
                left(halo.at[it, pl.ds(0, shards - 1)], halo_send.at[it])

            def summed(k):
                pltpu.make_async_copy(sum_src.at[it], sum_src.at[it], sum_send.at[it, k]).wait()

            nearest(summed)

            @pl.when(z + NEAR < depth)
            def _():
                pltpu.make_async_copy(run_src.at[it], run_src.at[it], run_send.at[it]).wait()

    offset = None
    for it in range(ITERS):
        lax.fori_loop(0, FINE, fine_step, 0, unroll=FINE)
        offset = flat(state[pl.ds(mine, 1)][0]) - coarse[...] * start[...]
        off_src[it] = offset.reshape(group, OCTET, cells)

        def off_copy(q):
            return pltpu.make_async_remote_copy(
                src_ref=off_src.at[it, q], dst_ref=offs.at[it, j], send_sem=off_send.at[it],
                recv_sem=off_recv.at[it], device_id=group_peer(q), device_id_type=MESH)

        others(group, j, lambda q: off_copy(q).start())
        offs[it, pl.ds(j, 1)] = off_src[it, pl.ds(j, 1)]
        if it == 0:
            def fill_gain(k, carry):
                z_gain[k] = jnp.exp(-(octet_column(z_rates[k]) * own_scale))
                return carry

            lax.fori_loop(first_near, z, fill_gain, 0)
            own_init = init_ref[pl.ds(pl.multiple_of(first_mode, OCTET), OCTET), :]
            since = ahead_of
            for q in range(group):
                plane_guess[q] = jnp.exp(-(octet_column(since) * own_scale)) * own_init
                since = since + group_rates[q]
        arrived(offs.at[it, pl.ds(0, group - 1)], off_recv.at[it])
        part = offs[it, 0]
        for q in range(1, group):
            part = group_gain[q] * part + offs[it, q]
        sum_src[it] = part

        def sum_copy(k, slot):
            return pltpu.make_async_remote_copy(
                src_ref=sum_src.at[it], dst_ref=sums.at[it, slot], send_sem=sum_send.at[it, k],
                recv_sem=sum_recv.at[it, slot], device_id=z_peer(k), device_id_type=MESH)

        nearest(lambda k: sum_copy(k, z).start())

        def run_copy():
            return pltpu.make_async_remote_copy(
                src_ref=run_src.at[it], dst_ref=run_dst.at[it], send_sem=run_send.at[it],
                recv_sem=run_recv.at[it], device_id=z_peer(z + NEAR), device_id_type=MESH)

        run_src[it] = jnp.zeros((OCTET, cells), jnp.float32)

        @pl.when(z >= NEAR)
        def _():
            run_copy().wait_recv()
            run_src[it] = run_dst[it]

        def add_sum(k, carried):
            sum_copy(k, k).wait_recv()
            return z_gain[k] * carried + sums[it, k]

        carried = lax.fori_loop(first_near, z, add_sum, run_src[it])
        for q in range(group):
            back_src[it, q] = carried
            carried = group_gain[q] * carried + offs[it, q]
        run_src[it] = carried

        @pl.when(z + NEAR < depth)
        def _():
            run_copy().start()

        def back_copy(q):
            return pltpu.make_async_remote_copy(
                src_ref=back_src.at[it, q], dst_ref=back.at[it, j], send_sem=back_send.at[it],
                recv_sem=back_recv.at[it], device_id=group_peer(q), device_id_type=MESH)

        if it + 1 < ITERS:
            for q in range(group):
                piece = plane_guess[q] + back_src[it, q]
                piece = jnp.concatenate([piece[:, n * LAYER : (n + 1) * LAYER] for n in range(2)], axis=0)
                halo_src[it, q] = piece.astype(jnp.bfloat16)

            def fan(p):
                others(group, j, lambda q: halo_copy(it, q, p).start())
                halo_copy(it, j, p).start()

            others(shards, mine, fan)

        others(group, j, lambda q: back_copy(q).start())
        back[it, pl.ds(j, 1)] = back_src[it, pl.ds(j, 1)]
        if it + 1 == ITERS:
            leave()
        arrived(back.at[it, pl.ds(0, group - 1)], back_recv.at[it])
        correction = back[it].reshape(DOF, cells)
        following = guess_at[...] + correction
        if it + 1 < ITERS:
            start[...] = following
            arrived(halo.at[it, pl.ds(0, shards - 1)], halo_recv.at[it])
            for p in range(shards):
                pieces = [halo[it, p, q].astype(jnp.float32) for q in range(group)]
                state[p] = jnp.concatenate(
                    [piece[:OCTET] for piece in pieces] + [piece[OCTET:] for piece in pieces], axis=0).T
            state[pl.ds(mine, 1)] = tall(following)[None]
        else:
            end = 0.5 * (coarse[...] * following + offset)
            sum_ref[...] = end + 0.5 * guess_at[...]
            difference_ref[...] = end - 0.5 * guess_at[...]
            arrived(back_src.at[it, pl.ds(0, group - 1)], back_send.at[it])


def per_device(depth, group, initial_state, inv_mass, element_scale, mode_rate, volume_block, face_blocks):
    shards = lax.axis_size("space")
    cells = initial_state.shape[1]
    f32, bf16 = jnp.float32, jnp.bfloat16
    vmem = pl.BlockSpec(memory_space=pltpu.VMEM)
    hbm = pl.BlockSpec(memory_space=pltpu.HBM)
    dma = pltpu.SemaphoreType.DMA
    half_sum, half_difference = pl.pallas_call(
        functools.partial(kernel, depth, group, shards),
        out_shape=[pltpu.VMEM((DOF, cells), f32)] * 2,
        in_specs=[hbm] * 6,
        out_specs=[vmem] * 2,
        scratch_shapes=[
            pltpu.VMEM((DOF, cells), f32),
            pltpu.VMEM((1, cells), f32),
            pltpu.VMEM((1, cells), f32),
            pltpu.VMEM((1, DOF), f32),
            pltpu.VMEM((DOF, DOF), bf16),
            pltpu.VMEM((6, DOF, DOF), bf16),
            pltpu.VMEM((12 * DOF, 2 * DOF), bf16),
            pltpu.VMEM((shards, LAYER, 2 * DOF), f32),
            pltpu.VMEM((shards, LAYER, 2 * DOF), f32),
            pltpu.VMEM((shards, LAYER, 2 * DOF), f32),
            pltpu.VMEM((DOF, cells), f32),
            pltpu.VMEM((DOF, cells), f32),
            pltpu.VMEM((DOF, cells), f32),
            pltpu.VMEM((shards, DOF, cells), f32),
            pltpu.VMEM((group, OCTET, cells), f32),
            pltpu.VMEM((ITERS - 1, group, 2 * OCTET, LAYER), bf16),
            pltpu.VMEM((ITERS - 1, shards, group, 2 * OCTET, LAYER), bf16),
            pltpu.VMEM((shards, 8, cells), f32),
            pltpu.VMEM((8, cells), f32),
            pltpu.VMEM((1, 128), f32),
            pltpu.VMEM((group, 1, 128), f32),
            pltpu.VMEM((1, 128), f32),
            pltpu.VMEM((depth, 1, 128), f32),
            pltpu.VMEM((1, 128), f32),
            pltpu.VMEM((1, 128), f32),
            pltpu.VMEM((group, OCTET, cells), f32),
            pltpu.VMEM((depth, OCTET, cells), f32),
            pltpu.VMEM((ITERS, group, OCTET, cells), f32),
            pltpu.VMEM((ITERS, group, OCTET, cells), f32),
            pltpu.VMEM((ITERS, OCTET, cells), f32),
            pltpu.VMEM((ITERS, depth, OCTET, cells), f32),
            pltpu.VMEM((ITERS, OCTET, cells), f32),
            pltpu.VMEM((ITERS, OCTET, cells), f32),
            pltpu.VMEM((ITERS, group, OCTET, cells), f32),
            pltpu.VMEM((ITERS, group, OCTET, cells), f32),
            dma((6,)), pltpu.SemaphoreType.REGULAR((depth,)), dma, dma, dma((depth,)), dma((depth,)), dma, dma,
            dma, dma, dma((ITERS,)), dma((ITERS,)),
            dma, dma, dma((ITERS,)), dma((ITERS,)),
            dma((ITERS, depth)), dma((ITERS, depth)), dma((ITERS,)), dma((ITERS,)), dma((ITERS,)), dma((ITERS,)),
        ],
        compiler_params=pltpu.CompilerParams(collective_id=1, has_side_effects=True),
        name="parareal",
    )(initial_state, inv_mass[None], element_scale[None], mode_rate, volume_block, face_blocks)
    return (half_sum + half_difference)[None], (half_sum - half_difference)[None]


def solution(mesh):
    slices = mesh.shape["tm"]
    group = DOF // OCTET
    placed = (P(None, "space"), P("space"), P("space"), P("tm", None), P(), P())
    return jax.shard_map(
        functools.partial(per_device, slices // group, group),
        mesh=mesh,
        in_specs=placed,
        out_specs=(P("tm", None, "space"), P("tm", None, "space")),
        check_vma=False,
    )
```

```python
import functools

import jax
import jax.numpy as jnp
from jax import lax
from jax.experimental import pallas as pl
from jax.experimental.pallas import tpu as pltpu
from jax.sharding import PartitionSpec as P

DOF = 64
EY = 16
EZ = 8
FINE = 8
ITERS = 2
LAYER = EY * EZ
OCTET = 8
NEAR = 4
MESH = pl.DeviceIdType.MESH


def kernel(
    depth, group, shards,
    init_hbm, mass_hbm, scale_hbm, rate_hbm, volume_hbm, faces_hbm,
    sum_ref, difference_ref,
    init_ref, mass_ref, scale_ref, rate_ref, volume_ref, faces_ref,
    blocks, state, decay, mass, coarse, guess_at, start, full, plane_guess, halo_src, halo, rows, row_src,
    rate_src, group_rates, tot_src, z_rates, pre_src, pre_dst,
    group_gain, z_gain, off_src, offs, sum_src, sums, run_src, run_dst, back_src, back,
    load, ready, rate_send, rate_recv, tot_send, tot_recv, pre_send, pre_recv, full_send, full_recv, halo_send, halo_recv,
    row_send, row_recv, off_send, off_recv, sum_send, sum_recv, run_send, run_recv, back_send, back_recv,
):
    cells = init_ref.shape[1]
    time = lax.axis_index("tm")
    mine = lax.axis_index("space")
    z = time // group
    j = lax.rem(time, group)

    def group_peer(q):
        return (z * group + q, mine)

    def z_peer(k):
        return (k * group + j, mine)

    def space_peer(p):
        return (time, p)

    half = group // 2
    moves = [(a, b) for a in range(2) for b in range(half)]
    moves = sorted(moves, key=lambda move: -(move[0] + min(move[1], half - move[1])))

    def plane_others(body):
        for a, b in moves:
            if a + b:
                body(lax.rem(j // half + a, 2) * half + lax.rem(lax.rem(j, half) + b, half))

    def slice_others(body):
        side, core = mine // 2, lax.rem(mine, 2)
        rest = lax.rem(side + 1, shards // 2) * 2
        body(rest + core)
        body(rest + 1 - core)
        body(side * 2 + 1 - core)

    def nearest(body):
        for d in range(1, NEAR):
            pl.when(z + d < depth)(functools.partial(body, z + d))

    def greet(peer):
        pl.semaphore_signal(barrier, inc=1, device_id=peer, device_id_type=MESH)

    def arrived(ref, sem):
        pltpu.make_async_copy(ref, ref, sem).wait()

    barrier = pltpu.get_barrier_semaphore()
    first_near = jnp.maximum(z - NEAR + 1, 0)
    plane_others(lambda q: greet(group_peer(q)))
    slice_others(lambda p: greet(space_peer(p)))
    lax.fori_loop(z + 1, jnp.minimum(z + NEAR + 1, depth), lambda k, c: (greet(z_peer(k)), c)[1], 0)

    loads = [
        pltpu.make_async_copy(src, dst, load.at[n])
        for n, (src, dst) in enumerate([
            (rate_hbm, rate_ref), (scale_hbm, scale_ref), (mass_hbm, mass_ref),
            (init_hbm, init_ref), (volume_hbm, volume_ref), (faces_hbm, faces_ref),
        ])
    ]
    for copy in loads:
        copy.start()

    sub = lax.broadcasted_iota(jnp.int32, (DOF, 128), 0)
    lane = lax.broadcasted_iota(jnp.int32, (DOF, 128), 1)
    sub_o = lax.broadcasted_iota(jnp.int32, (OCTET, 128), 0)
    lane_o = lax.broadcasted_iota(jnp.int32, (OCTET, 128), 1)
    first_mode = OCTET * j

    def column(values):
        return jnp.sum(jnp.where(sub == lane, values, 0.0), axis=1, keepdims=True)

    def octet_column(values):
        return jnp.sum(jnp.where(lane_o == sub_o + first_mode, values, 0.0), axis=1, keepdims=True)

    for copy in loads:
        copy.wait()
    row = jnp.concatenate([rate_ref[...], jnp.zeros((1, 128 - DOF), jnp.float32)], axis=1)
    rate_src[...] = row
    group_rates[pl.ds(j, 1)] = row[None]
    row_src[...] = jnp.concatenate(
        [mass_ref[...], scale_ref[...], jnp.zeros((6, cells), jnp.float32)], axis=0
    )
    rows[pl.ds(mine, 1)] = row_src[...][None]
    full[pl.ds(mine, 1)] = init_ref[...][None]
    turned = [volume_ref[...]] + [faces_ref[f] for f in range(6)]
    turned = [block.astype(jnp.float32).T.astype(jnp.bfloat16) for block in turned]
    none = jnp.zeros((DOF, DOF), jnp.bfloat16)
    grid = [[turned[0], turned[1]], [turned[2], turned[0]], [none, turned[2]], [turned[1], none]]
    for f in range(3, 7):
        grid += [[turned[f], none], [none, turned[f]]]
    for n, (left_block, right_block) in enumerate(grid):
        blocks[DOF * n : DOF * (n + 1), :DOF] = left_block
        blocks[DOF * n : DOF * (n + 1), DOF:] = right_block

    def tall(value):
        return jnp.concatenate([value[:, :LAYER], value[:, LAYER:]], axis=0).T

    def flat(value):
        value = value.T
        return jnp.concatenate([value[:DOF], value[DOF:]], axis=1)

    own_scale = scale_ref[...]
    own_column = column(row)
    coarse[...] = jnp.exp(-(own_column * own_scale))

    pl.semaphore_wait(barrier, group + shards - 2 + jnp.minimum(z, NEAR))

    def rate_copy(q):
        return pltpu.make_async_remote_copy(
            src_ref=rate_src, dst_ref=group_rates.at[j], send_sem=rate_send, recv_sem=rate_recv,
            device_id=group_peer(q), device_id_type=MESH)

    def full_copy(p):
        return pltpu.make_async_remote_copy(
            src_ref=init_ref, dst_ref=full.at[mine], send_sem=full_send, recv_sem=full_recv,
            device_id=space_peer(p), device_id_type=MESH)

    def halo_copy(it, q, p):
        return pltpu.make_async_remote_copy(
            src_ref=halo_src.at[it, q], dst_ref=halo.at[it, mine, j], send_sem=halo_send.at[it],
            recv_sem=halo_recv.at[it], device_id=(z * group + q, p), device_id_type=MESH)

    def row_copy(p):
        return pltpu.make_async_remote_copy(
            src_ref=row_src, dst_ref=rows.at[mine], send_sem=row_send, recv_sem=row_recv,
            device_id=space_peer(p), device_id_type=MESH)

    plane_others(lambda q: rate_copy(q).start())
    lax.fori_loop(
        0, jnp.minimum(z, NEAR),
        lambda k, c: (
            pl.semaphore_signal(ready.at[z], inc=1, device_id=z_peer(z - 1 - k), device_id_type=MESH), c)[1], 0)
    slice_others(lambda p: row_copy(p).start())
    slice_others(lambda p: full_copy(p).start())
    arrived(group_rates.at[pl.ds(0, group - 1)], rate_recv)
    total = jnp.zeros((1, 128), jnp.float32)
    before = jnp.zeros((1, 128), jnp.float32)
    for q in range(group):
        before = before + jnp.where(q < j, group_rates[q], 0.0)
        total = total + group_rates[q]
    tot_src[...] = total

    def tot_copy(k, slot):
        return pltpu.make_async_remote_copy(
            src_ref=tot_src, dst_ref=z_rates.at[slot], send_sem=tot_send.at[k], recv_sem=tot_recv.at[slot],
            device_id=z_peer(k), device_id_type=MESH)

    def tell(k, carry):
        pl.semaphore_wait(ready.at[k], 1)
        tot_copy(k, z).start()
        return carry

    lax.fori_loop(z + 1, jnp.minimum(z + 2, depth), tell, 0)

    for q in range(group):
        group_gain[q] = jnp.exp(-(octet_column(group_rates[q]) * own_scale))
    arrived(rows.at[pl.ds(0, shards - 1)], row_recv)
    for p in range(shards):
        decay[p] = tall(jnp.exp(-(own_column * rows[p, 1:2, :]) / FINE))
        mass[p] = tall(jnp.broadcast_to(rows[p, 0:1, :], (DOF, cells)))
    arrived(full.at[pl.ds(0, shards - 1)], full_recv)

    def pre_copy():
        return pltpu.make_async_remote_copy(
            src_ref=pre_src, dst_ref=pre_dst, send_sem=pre_send, recv_sem=pre_recv,
            device_id=z_peer(z + NEAR), device_id_type=MESH)

    lax.fori_loop(z + 2, jnp.minimum(z + NEAR, depth), tell, 0)

    pre_src[...] = jnp.zeros((1, 128), jnp.float32)

    @pl.when(z >= NEAR)
    def _():
        pre_copy().wait_recv()
        pre_src[...] = pre_dst[...]

    def add_total(k, carried):
        tot_copy(k, k).wait_recv()
        return carried + z_rates[k]

    ahead_of = lax.fori_loop(first_near, z, add_total, pre_src[...])
    pre_src[...] = ahead_of + total

    @pl.when(z + NEAR < depth)
    def _():
        pl.semaphore_wait(ready.at[z + NEAR], 1)
        pre_copy().start()

    passed = column(ahead_of + before)
    for p in range(shards):
        state[p] = tall(jnp.exp(-(passed * rows[p, 1:2, :])) * full[p])
    guess = jnp.exp(-(passed * own_scale)) * init_ref[...]
    guess_at[...] = guess
    start[...] = guess

    low = lax.broadcasted_iota(jnp.int32, (LAYER, 2 * DOF), 1) < DOF

    def turn(value, by):
        return pltpu.roll(value.reshape(EY, EZ, 2 * DOF), by, 1).reshape(LAYER, 2 * DOF)

    def advanced(value, after, before_it, value_decay, value_mass):
        beside = jnp.where(low, after, before_it)
        parts = [
            value, beside, pltpu.roll(value, EZ, 0), pltpu.roll(value, LAYER - EZ, 0),
            turn(value, 1), turn(value, EZ - 1),
        ]
        stacked = jnp.concatenate([part.astype(jnp.bfloat16) for part in parts], axis=1)
        change = jnp.dot(stacked, blocks[...], preferred_element_type=jnp.float32)
        return value_decay * value + value_mass * change

    def fine_step(step, carry):
        old = [state[p] for p in range(shards)]
        edge = jnp.zeros((LAYER, 2 * DOF), jnp.float32)
        for p in range(shards):
            after = old[p + 1] if p + 1 < shards else edge
            state[p] = advanced(old[p], after, old[p - 1] if p else edge, decay[p], mass[p])
        return carry

    def at(ref, p):
        return ref[pl.ds(p, 1)][0]

    def last_step():
        after = jnp.where(mine + 1 < shards, at(state, jnp.minimum(mine + 1, shards - 1)), 0.0)
        before_it = jnp.where(mine > 0, at(state, jnp.maximum(mine - 1, 0)), 0.0)
        return advanced(at(state, mine), after, before_it, at(decay, mine), at(mass, mine))

    def leave():
        def left(ref, sem):
            pltpu.make_async_copy(ref, ref, sem).wait()

        left(group_rates.at[pl.ds(0, group - 1)], rate_send)
        left(rows.at[pl.ds(0, shards - 1)], row_send)
        left(full.at[pl.ds(0, shards - 1)], full_send)
        nearest(lambda k: tot_copy(k, z).wait_send())

        @pl.when(z + NEAR < depth)
        def _():
            pre_copy().wait_send()

        for it in range(ITERS):
            left(off_src.at[it, pl.ds(0, group - 1)], off_send.at[it])
            if it + 1 < ITERS:
                left(back_src.at[it, pl.ds(0, group - 1)], back_send.at[it])
            if it + 1 < ITERS:
                left(halo.at[it, pl.ds(0, shards - 1)], halo_send.at[it])

            def summed(k):
                pltpu.make_async_copy(sum_src.at[it], sum_src.at[it], sum_send.at[it, k]).wait()

            nearest(summed)

            @pl.when(z + NEAR < depth)
            def _():
                pltpu.make_async_copy(run_src.at[it], run_src.at[it], run_send.at[it]).wait()

    offset = None
    for it in range(ITERS):
        lax.fori_loop(0, FINE - 1, fine_step, 0, unroll=FINE - 1)
        offset = flat(last_step()) - coarse[...] * start[...]
        off_src[it] = offset.reshape(group, OCTET, cells)

        def off_copy(q):
            return pltpu.make_async_remote_copy(
                src_ref=off_src.at[it, q], dst_ref=offs.at[it, j], send_sem=off_send.at[it],
                recv_sem=off_recv.at[it], device_id=group_peer(q), device_id_type=MESH)

        plane_others(lambda q: off_copy(q).start())
        offs[it, pl.ds(j, 1)] = off_src[it, pl.ds(j, 1)]
        if it == 0:
            def fill_gain(k, carry):
                z_gain[k] = jnp.exp(-(octet_column(z_rates[k]) * own_scale))
                return carry

            lax.fori_loop(first_near, z, fill_gain, 0)
            own_init = init_ref[pl.ds(pl.multiple_of(first_mode, OCTET), OCTET), :]
            since = ahead_of
            for q in range(group):
                plane_guess[q] = jnp.exp(-(octet_column(since) * own_scale)) * own_init
                since = since + group_rates[q]
        arrived(offs.at[it, pl.ds(0, group - 1)], off_recv.at[it])
        part = offs[it, 0]
        for q in range(1, group):
            part = group_gain[q] * part + offs[it, q]
        sum_src[it] = part

        def sum_copy(k, slot):
            return pltpu.make_async_remote_copy(
                src_ref=sum_src.at[it], dst_ref=sums.at[it, slot], send_sem=sum_send.at[it, k],
                recv_sem=sum_recv.at[it, slot], device_id=z_peer(k), device_id_type=MESH)

        nearest(lambda k: sum_copy(k, z).start())

        def run_copy():
            return pltpu.make_async_remote_copy(
                src_ref=run_src.at[it], dst_ref=run_dst.at[it], send_sem=run_send.at[it],
                recv_sem=run_recv.at[it], device_id=z_peer(z + NEAR), device_id_type=MESH)

        run_src[it] = jnp.zeros((OCTET, cells), jnp.float32)

        @pl.when(z >= NEAR)
        def _():
            run_copy().wait_recv()
            run_src[it] = run_dst[it]

        def add_sum(k, carried):
            sum_copy(k, k).wait_recv()
            return z_gain[k] * carried + sums[it, k]

        carried = lax.fori_loop(first_near, z, add_sum, run_src[it])
        for q in range(group):
            back_src[it, q] = carried
            carried = group_gain[q] * carried + offs[it, q]
        run_src[it] = carried

        @pl.when(z + NEAR < depth)
        def _():
            run_copy().start()

        def back_copy(q):
            return pltpu.make_async_remote_copy(
                src_ref=back_src.at[it, q], dst_ref=back.at[it, j], send_sem=back_send.at[it],
                recv_sem=back_recv.at[it], device_id=group_peer(q), device_id_type=MESH)

        if it + 1 < ITERS:
            for q in range(group):
                piece = plane_guess[q] + back_src[it, q]
                piece = jnp.concatenate([piece[:, n * LAYER : (n + 1) * LAYER] for n in range(2)], axis=0)
                halo_src[it, q] = piece.astype(jnp.bfloat16)

            def fan(p):
                plane_others(lambda q: halo_copy(it, q, p).start())
                halo_copy(it, j, p).start()

            slice_others(fan)

        plane_others(lambda q: back_copy(q).start())
        back[it, pl.ds(j, 1)] = back_src[it, pl.ds(j, 1)]
        if it + 1 == ITERS:
            leave()
        arrived(back.at[it, pl.ds(0, group - 1)], back_recv.at[it])
        correction = back[it].reshape(DOF, cells)
        following = guess_at[...] + correction
        if it + 1 < ITERS:
            start[...] = following
            arrived(halo.at[it, pl.ds(0, shards - 1)], halo_recv.at[it])
            for p in range(shards):
                pieces = [halo[it, p, q].astype(jnp.float32) for q in range(group)]
                state[p] = jnp.concatenate(
                    [piece[:OCTET] for piece in pieces] + [piece[OCTET:] for piece in pieces], axis=0).T
            state[pl.ds(mine, 1)] = tall(following)[None]
        else:
            end = 0.5 * (coarse[...] * following + offset)
            sum_ref[...] = end + 0.5 * guess_at[...]
            difference_ref[...] = end - 0.5 * guess_at[...]
            arrived(back_src.at[it, pl.ds(0, group - 1)], back_send.at[it])


def per_device(depth, group, initial_state, inv_mass, element_scale, mode_rate, volume_block, face_blocks):
    shards = lax.axis_size("space")
    cells = initial_state.shape[1]
    f32, bf16 = jnp.float32, jnp.bfloat16
    vmem = pl.BlockSpec(memory_space=pltpu.VMEM)
    hbm = pl.BlockSpec(memory_space=pltpu.HBM)
    dma = pltpu.SemaphoreType.DMA
    half_sum, half_difference = pl.pallas_call(
        functools.partial(kernel, depth, group, shards),
        out_shape=[pltpu.VMEM((DOF, cells), f32)] * 2,
        in_specs=[hbm] * 6,
        out_specs=[vmem] * 2,
        scratch_shapes=[
            pltpu.VMEM((DOF, cells), f32),
            pltpu.VMEM((1, cells), f32),
            pltpu.VMEM((1, cells), f32),
            pltpu.VMEM((1, DOF), f32),
            pltpu.VMEM((DOF, DOF), bf16),
            pltpu.VMEM((6, DOF, DOF), bf16),
            pltpu.VMEM((12 * DOF, 2 * DOF), bf16),
            pltpu.VMEM((shards, LAYER, 2 * DOF), f32),
            pltpu.VMEM((shards, LAYER, 2 * DOF), f32),
            pltpu.VMEM((shards, LAYER, 2 * DOF), f32),
            pltpu.VMEM((DOF, cells), f32),
            pltpu.VMEM((DOF, cells), f32),
            pltpu.VMEM((DOF, cells), f32),
            pltpu.VMEM((shards, DOF, cells), f32),
            pltpu.VMEM((group, OCTET, cells), f32),
            pltpu.VMEM((ITERS - 1, group, 2 * OCTET, LAYER), bf16),
            pltpu.VMEM((ITERS - 1, shards, group, 2 * OCTET, LAYER), bf16),
            pltpu.VMEM((shards, 8, cells), f32),
            pltpu.VMEM((8, cells), f32),
            pltpu.VMEM((1, 128), f32),
            pltpu.VMEM((group, 1, 128), f32),
            pltpu.VMEM((1, 128), f32),
            pltpu.VMEM((depth, 1, 128), f32),
            pltpu.VMEM((1, 128), f32),
            pltpu.VMEM((1, 128), f32),
            pltpu.VMEM((group, OCTET, cells), f32),
            pltpu.VMEM((depth, OCTET, cells), f32),
            pltpu.VMEM((ITERS, group, OCTET, cells), f32),
            pltpu.VMEM((ITERS, group, OCTET, cells), f32),
            pltpu.VMEM((ITERS, OCTET, cells), f32),
            pltpu.VMEM((ITERS, depth, OCTET, cells), f32),
            pltpu.VMEM((ITERS, OCTET, cells), f32),
            pltpu.VMEM((ITERS, OCTET, cells), f32),
            pltpu.VMEM((ITERS, group, OCTET, cells), f32),
            pltpu.VMEM((ITERS, group, OCTET, cells), f32),
            dma((6,)), pltpu.SemaphoreType.REGULAR((depth,)), dma, dma, dma((depth,)), dma((depth,)), dma, dma,
            dma, dma, dma((ITERS,)), dma((ITERS,)),
            dma, dma, dma((ITERS,)), dma((ITERS,)),
            dma((ITERS, depth)), dma((ITERS, depth)), dma((ITERS,)), dma((ITERS,)), dma((ITERS,)), dma((ITERS,)),
        ],
        compiler_params=pltpu.CompilerParams(collective_id=1, has_side_effects=True),
        name="parareal",
    )(initial_state, inv_mass[None], element_scale[None], mode_rate, volume_block, face_blocks)
    return (half_sum + half_difference)[None], (half_sum - half_difference)[None]


def solution(mesh):
    slices = mesh.shape["tm"]
    group = DOF // OCTET
    placed = (P(None, "space"), P("space"), P("space"), P("tm", None), P(), P())
    return jax.shard_map(
        functools.partial(per_device, slices // group, group),
        mesh=mesh,
        in_specs=placed,
        out_specs=(P("tm", None, "space"), P("tm", None, "space")),
        check_vma=False,
    )
```

```python
import functools

import jax
import jax.numpy as jnp
from jax import lax
from jax.experimental import pallas as pl
from jax.experimental.pallas import tpu as pltpu
from jax.sharding import PartitionSpec as P

DOF = 64
EY = 16
EZ = 8
FINE = 8
ITERS = 2
LAYER = EY * EZ
OCTET = 8
NEAR = 4
MESH = pl.DeviceIdType.MESH


def kernel(
    depth, group, shards,
    init_hbm, mass_hbm, scale_hbm, rate_hbm, volume_hbm, faces_hbm,
    sum_ref, difference_ref,
    init_ref, mass_ref, scale_ref, rate_ref, volume_ref, faces_ref,
    blocks, state, decay, mass, coarse, guess_at, start, full, plane_guess, halo_src, halo, rows, row_src,
    rate_src, group_rates, tot_src, z_rates, pre_src, pre_dst,
    group_gain, z_gain, off_src, offs, sum_src, sums, run_src, run_dst, back_src, back,
    load, ready, rate_send, rate_recv, tot_send, tot_recv, pre_send, pre_recv, full_send, full_recv, halo_send, halo_recv,
    row_send, row_recv, off_send, off_recv, sum_send, sum_recv, run_send, run_recv, back_send, back_recv,
):
    cells = init_ref.shape[1]
    time = lax.axis_index("tm")
    mine = lax.axis_index("space")
    z = time // group
    j = lax.rem(time, group)

    def group_peer(q):
        return (z * group + q, mine)

    def z_peer(k):
        return (k * group + j, mine)

    def space_peer(p):
        return (time, p)

    half = group // 2
    moves = [(a, b) for a in range(2) for b in range(half)]
    moves = sorted(moves, key=lambda move: -(move[0] + min(move[1], half - move[1])))

    def plane_others(body):
        for a, b in moves:
            if a + b:
                body(lax.rem(j // half + a, 2) * half + lax.rem(lax.rem(j, half) + b, half))

    def slice_others(body):
        side, core = mine // 2, lax.rem(mine, 2)
        rest = lax.rem(side + 1, shards // 2) * 2
        body(rest + core)
        body(rest + 1 - core)
        body(side * 2 + 1 - core)

    def nearest(body):
        for d in range(1, NEAR):
            pl.when(z + d < depth)(functools.partial(body, z + d))

    def greet(peer):
        pl.semaphore_signal(barrier, inc=1, device_id=peer, device_id_type=MESH)

    def arrived(ref, sem):
        pltpu.make_async_copy(ref, ref, sem).wait()

    barrier = pltpu.get_barrier_semaphore()
    first_near = jnp.maximum(z - NEAR + 1, 0)
    plane_others(lambda q: greet(group_peer(q)))
    slice_others(lambda p: greet(space_peer(p)))
    lax.fori_loop(z + 1, jnp.minimum(z + NEAR + 1, depth), lambda k, c: (greet(z_peer(k)), c)[1], 0)

    loads = [
        pltpu.make_async_copy(src, dst, load.at[n])
        for n, (src, dst) in enumerate([
            (rate_hbm, rate_ref), (scale_hbm, scale_ref), (mass_hbm, mass_ref),
            (init_hbm, init_ref), (volume_hbm, volume_ref), (faces_hbm, faces_ref),
        ])
    ]
    for copy in loads:
        copy.start()

    sub = lax.broadcasted_iota(jnp.int32, (DOF, 128), 0)
    lane = lax.broadcasted_iota(jnp.int32, (DOF, 128), 1)
    sub_o = lax.broadcasted_iota(jnp.int32, (OCTET, 128), 0)
    lane_o = lax.broadcasted_iota(jnp.int32, (OCTET, 128), 1)
    first_mode = OCTET * j

    def column(values):
        return jnp.sum(jnp.where(sub == lane, values, 0.0), axis=1, keepdims=True)

    def octet_column(values):
        return jnp.sum(jnp.where(lane_o == sub_o + first_mode, values, 0.0), axis=1, keepdims=True)

    for copy in loads:
        copy.wait()
    row = jnp.concatenate([rate_ref[...], jnp.zeros((1, 128 - DOF), jnp.float32)], axis=1)
    rate_src[...] = row
    group_rates[pl.ds(j, 1)] = row[None]
    row_src[...] = jnp.concatenate(
        [mass_ref[...], scale_ref[...], jnp.zeros((6, cells), jnp.float32)], axis=0
    )
    rows[pl.ds(mine, 1)] = row_src[...][None]
    full[pl.ds(mine, 1)] = init_ref[...][None]
    turned = [volume_ref[...]] + [faces_ref[f] for f in range(6)]
    turned = [block.astype(jnp.float32).T.astype(jnp.bfloat16) for block in turned]
    none = jnp.zeros((DOF, DOF), jnp.bfloat16)
    grid = [[turned[0], turned[1]], [turned[2], turned[0]], [none, turned[2]], [turned[1], none]]
    for f in range(3, 7):
        grid += [[turned[f], none], [none, turned[f]]]
    for n, (left_block, right_block) in enumerate(grid):
        blocks[DOF * n : DOF * (n + 1), :DOF] = left_block
        blocks[DOF * n : DOF * (n + 1), DOF:] = right_block

    def tall(value):
        return jnp.concatenate([value[:, :LAYER], value[:, LAYER:]], axis=0).T

    def flat(value):
        value = value.T
        return jnp.concatenate([value[:DOF], value[DOF:]], axis=1)

    own_scale = scale_ref[...]
    own_column = column(row)
    coarse[...] = jnp.exp(-(own_column * own_scale))

    pl.semaphore_wait(barrier, group + shards - 2 + jnp.minimum(z, NEAR))

    def rate_copy(q):
        return pltpu.make_async_remote_copy(
            src_ref=rate_src, dst_ref=group_rates.at[j], send_sem=rate_send, recv_sem=rate_recv,
            device_id=group_peer(q), device_id_type=MESH)

    def full_copy(p):
        return pltpu.make_async_remote_copy(
            src_ref=init_ref, dst_ref=full.at[mine], send_sem=full_send, recv_sem=full_recv,
            device_id=space_peer(p), device_id_type=MESH)

    def halo_copy(it, q, p):
        return pltpu.make_async_remote_copy(
            src_ref=halo_src.at[it, q], dst_ref=halo.at[it, mine, j], send_sem=halo_send.at[it],
            recv_sem=halo_recv.at[it], device_id=(z * group + q, p), device_id_type=MESH)

    def row_copy(p):
        return pltpu.make_async_remote_copy(
            src_ref=row_src, dst_ref=rows.at[mine], send_sem=row_send, recv_sem=row_recv,
            device_id=space_peer(p), device_id_type=MESH)

    lax.fori_loop(
        0, jnp.minimum(z, NEAR),
        lambda k, c: (
            pl.semaphore_signal(ready.at[z], inc=1, device_id=z_peer(z - 1 - k), device_id_type=MESH), c)[1], 0)
    plane_others(lambda q: rate_copy(q).start())
    slice_others(lambda p: row_copy(p).start())
    slice_others(lambda p: full_copy(p).start())
    arrived(group_rates.at[pl.ds(0, group - 1)], rate_recv)
    total = jnp.zeros((1, 128), jnp.float32)
    before = jnp.zeros((1, 128), jnp.float32)
    for q in range(group):
        before = before + jnp.where(q < j, group_rates[q], 0.0)
        total = total + group_rates[q]
    tot_src[...] = total

    def tot_copy(k, slot):
        return pltpu.make_async_remote_copy(
            src_ref=tot_src, dst_ref=z_rates.at[slot], send_sem=tot_send.at[k], recv_sem=tot_recv.at[slot],
            device_id=z_peer(k), device_id_type=MESH)

    def tell(k, carry):
        pl.semaphore_wait(ready.at[k], 1)
        tot_copy(k, z).start()
        return carry

    lax.fori_loop(z + 1, jnp.minimum(z + 2, depth), tell, 0)

    for q in range(group):
        group_gain[q] = jnp.exp(-(octet_column(group_rates[q]) * own_scale))
    arrived(rows.at[pl.ds(0, shards - 1)], row_recv)
    for p in range(shards):
        decay[p] = tall(jnp.exp(-(own_column * rows[p, 1:2, :]) / FINE))
        mass[p] = tall(jnp.broadcast_to(rows[p, 0:1, :], (DOF, cells)))
    arrived(full.at[pl.ds(0, shards - 1)], full_recv)

    def pre_copy():
        return pltpu.make_async_remote_copy(
            src_ref=pre_src, dst_ref=pre_dst, send_sem=pre_send, recv_sem=pre_recv,
            device_id=z_peer(z + NEAR), device_id_type=MESH)

    lax.fori_loop(z + 2, jnp.minimum(z + NEAR, depth), tell, 0)

    pre_src[...] = jnp.zeros((1, 128), jnp.float32)

    @pl.when(z >= NEAR)
    def _():
        pre_copy().wait_recv()
        pre_src[...] = pre_dst[...]

    def add_total(k, carried):
        tot_copy(k, k).wait_recv()
        return carried + z_rates[k]

    ahead_of = lax.fori_loop(first_near, z, add_total, pre_src[...])
    pre_src[...] = ahead_of + total

    @pl.when(z + NEAR < depth)
    def _():
        pl.semaphore_wait(ready.at[z + NEAR], 1)
        pre_copy().start()

    passed = column(ahead_of + before)
    for p in range(shards):
        state[p] = tall(jnp.exp(-(passed * rows[p, 1:2, :])) * full[p])
    guess = jnp.exp(-(passed * own_scale)) * init_ref[...]
    guess_at[...] = guess
    start[...] = guess

    low = lax.broadcasted_iota(jnp.int32, (LAYER, 2 * DOF), 1) < DOF

    def turn(value, by):
        return pltpu.roll(value.reshape(EY, EZ, 2 * DOF), by, 1).reshape(LAYER, 2 * DOF)

    def advanced(value, after, before_it, value_decay, value_mass):
        beside = jnp.where(low, after, before_it)
        parts = [
            value, beside, pltpu.roll(value, EZ, 0), pltpu.roll(value, LAYER - EZ, 0),
            turn(value, 1), turn(value, EZ - 1),
        ]
        stacked = jnp.concatenate([part.astype(jnp.bfloat16) for part in parts], axis=1)
        change = jnp.dot(stacked, blocks[...], preferred_element_type=jnp.float32)
        return value_decay * value + value_mass * change

    def fine_step(step, carry):
        old = [state[p] for p in range(shards)]
        edge = jnp.zeros((LAYER, 2 * DOF), jnp.float32)
        for p in range(shards):
            after = old[p + 1] if p + 1 < shards else edge
            state[p] = advanced(old[p], after, old[p - 1] if p else edge, decay[p], mass[p])
        return carry

    def at(ref, p):
        return ref[pl.ds(p, 1)][0]

    def last_step():
        after = jnp.where(mine + 1 < shards, at(state, jnp.minimum(mine + 1, shards - 1)), 0.0)
        before_it = jnp.where(mine > 0, at(state, jnp.maximum(mine - 1, 0)), 0.0)
        return advanced(at(state, mine), after, before_it, at(decay, mine), at(mass, mine))

    def leave():
        def left(ref, sem):
            pltpu.make_async_copy(ref, ref, sem).wait()

        left(group_rates.at[pl.ds(0, group - 1)], rate_send)
        left(rows.at[pl.ds(0, shards - 1)], row_send)
        left(full.at[pl.ds(0, shards - 1)], full_send)
        nearest(lambda k: tot_copy(k, z).wait_send())

        @pl.when(z + NEAR < depth)
        def _():
            pre_copy().wait_send()

        for it in range(ITERS):
            left(off_src.at[it, pl.ds(0, group - 1)], off_send.at[it])
            if it + 1 < ITERS:
                left(back_src.at[it, pl.ds(0, group - 1)], back_send.at[it])
            if it + 1 < ITERS:
                left(halo.at[it, pl.ds(0, shards - 1)], halo_send.at[it])

            def summed(k):
                pltpu.make_async_copy(sum_src.at[it], sum_src.at[it], sum_send.at[it, k]).wait()

            nearest(summed)

            @pl.when(z + NEAR < depth)
            def _():
                pltpu.make_async_copy(run_src.at[it], run_src.at[it], run_send.at[it]).wait()

    offset = None
    for it in range(ITERS):
        lax.fori_loop(0, FINE - 1, fine_step, 0, unroll=FINE - 1)
        offset = flat(last_step()) - coarse[...] * start[...]
        off_src[it] = offset.reshape(group, OCTET, cells)

        def off_copy(q):
            return pltpu.make_async_remote_copy(
                src_ref=off_src.at[it, q], dst_ref=offs.at[it, j], send_sem=off_send.at[it],
                recv_sem=off_recv.at[it], device_id=group_peer(q), device_id_type=MESH)

        plane_others(lambda q: off_copy(q).start())
        offs[it, pl.ds(j, 1)] = off_src[it, pl.ds(j, 1)]
        if it == 0:
            def fill_gain(k, carry):
                z_gain[k] = jnp.exp(-(octet_column(z_rates[k]) * own_scale))
                return carry

            lax.fori_loop(first_near, z, fill_gain, 0)
            own_init = init_ref[pl.ds(pl.multiple_of(first_mode, OCTET), OCTET), :]
            since = ahead_of
            for q in range(group):
                plane_guess[q] = jnp.exp(-(octet_column(since) * own_scale)) * own_init
                since = since + group_rates[q]
        arrived(offs.at[it, pl.ds(0, group - 1)], off_recv.at[it])
        part = offs[it, 0]
        for q in range(1, group):
            part = group_gain[q] * part + offs[it, q]
        sum_src[it] = part

        def sum_copy(k, slot):
            return pltpu.make_async_remote_copy(
                src_ref=sum_src.at[it], dst_ref=sums.at[it, slot], send_sem=sum_send.at[it, k],
                recv_sem=sum_recv.at[it, slot], device_id=z_peer(k), device_id_type=MESH)

        nearest(lambda k: sum_copy(k, z).start())

        def run_copy():
            return pltpu.make_async_remote_copy(
                src_ref=run_src.at[it], dst_ref=run_dst.at[it], send_sem=run_send.at[it],
                recv_sem=run_recv.at[it], device_id=z_peer(z + NEAR), device_id_type=MESH)

        run_src[it] = jnp.zeros((OCTET, cells), jnp.float32)

        @pl.when(z >= NEAR)
        def _():
            run_copy().wait_recv()
            run_src[it] = run_dst[it]

        def add_sum(k, carried):
            sum_copy(k, k).wait_recv()
            return z_gain[k] * carried + sums[it, k]

        carried = lax.fori_loop(first_near, z, add_sum, run_src[it])
        for q in range(group):
            back_src[it, q] = carried
            carried = group_gain[q] * carried + offs[it, q]
        run_src[it] = carried

        @pl.when(z + NEAR < depth)
        def _():
            run_copy().start()

        def back_copy(q):
            return pltpu.make_async_remote_copy(
                src_ref=back_src.at[it, q], dst_ref=back.at[it, j], send_sem=back_send.at[it],
                recv_sem=back_recv.at[it], device_id=group_peer(q), device_id_type=MESH)

        if it + 1 < ITERS:
            for q in range(group):
                piece = plane_guess[q] + back_src[it, q]
                piece = jnp.concatenate([piece[:, n * LAYER : (n + 1) * LAYER] for n in range(2)], axis=0)
                halo_src[it, q] = piece.astype(jnp.bfloat16)

            def fan(p):
                plane_others(lambda q: halo_copy(it, q, p).start())
                halo_copy(it, j, p).start()

            slice_others(fan)

        plane_others(lambda q: back_copy(q).start())
        back[it, pl.ds(j, 1)] = back_src[it, pl.ds(j, 1)]
        if it + 1 == ITERS:
            leave()
        arrived(back.at[it, pl.ds(0, group - 1)], back_recv.at[it])
        correction = back[it].reshape(DOF, cells)
        following = guess_at[...] + correction
        if it + 1 < ITERS:
            start[...] = following
            arrived(halo.at[it, pl.ds(0, shards - 1)], halo_recv.at[it])
            for p in range(shards):
                pieces = [halo[it, p, q].astype(jnp.float32) for q in range(group)]
                state[p] = jnp.concatenate(
                    [piece[:OCTET] for piece in pieces] + [piece[OCTET:] for piece in pieces], axis=0).T
            state[pl.ds(mine, 1)] = tall(following)[None]
        else:
            end = 0.5 * (coarse[...] * following + offset)
            sum_ref[...] = end + 0.5 * guess_at[...]
            difference_ref[...] = end - 0.5 * guess_at[...]
            arrived(back_src.at[it, pl.ds(0, group - 1)], back_send.at[it])


def per_device(depth, group, initial_state, inv_mass, element_scale, mode_rate, volume_block, face_blocks):
    shards = lax.axis_size("space")
    cells = initial_state.shape[1]
    f32, bf16 = jnp.float32, jnp.bfloat16
    vmem = pl.BlockSpec(memory_space=pltpu.VMEM)
    hbm = pl.BlockSpec(memory_space=pltpu.HBM)
    dma = pltpu.SemaphoreType.DMA
    half_sum, half_difference = pl.pallas_call(
        functools.partial(kernel, depth, group, shards),
        out_shape=[pltpu.VMEM((DOF, cells), f32)] * 2,
        in_specs=[hbm] * 6,
        out_specs=[vmem] * 2,
        scratch_shapes=[
            pltpu.VMEM((DOF, cells), f32),
            pltpu.VMEM((1, cells), f32),
            pltpu.VMEM((1, cells), f32),
            pltpu.VMEM((1, DOF), f32),
            pltpu.VMEM((DOF, DOF), bf16),
            pltpu.VMEM((6, DOF, DOF), bf16),
            pltpu.VMEM((12 * DOF, 2 * DOF), bf16),
            pltpu.VMEM((shards, LAYER, 2 * DOF), f32),
            pltpu.VMEM((shards, LAYER, 2 * DOF), f32),
            pltpu.VMEM((shards, LAYER, 2 * DOF), f32),
            pltpu.VMEM((DOF, cells), f32),
            pltpu.VMEM((DOF, cells), f32),
            pltpu.VMEM((DOF, cells), f32),
            pltpu.VMEM((shards, DOF, cells), f32),
            pltpu.VMEM((group, OCTET, cells), f32),
            pltpu.VMEM((ITERS - 1, group, 2 * OCTET, LAYER), bf16),
            pltpu.VMEM((ITERS - 1, shards, group, 2 * OCTET, LAYER), bf16),
            pltpu.VMEM((shards, 8, cells), f32),
            pltpu.VMEM((8, cells), f32),
            pltpu.VMEM((1, 128), f32),
            pltpu.VMEM((group, 1, 128), f32),
            pltpu.VMEM((1, 128), f32),
            pltpu.VMEM((depth, 1, 128), f32),
            pltpu.VMEM((1, 128), f32),
            pltpu.VMEM((1, 128), f32),
            pltpu.VMEM((group, OCTET, cells), f32),
            pltpu.VMEM((depth, OCTET, cells), f32),
            pltpu.VMEM((ITERS, group, OCTET, cells), f32),
            pltpu.VMEM((ITERS, group, OCTET, cells), f32),
            pltpu.VMEM((ITERS, OCTET, cells), f32),
            pltpu.VMEM((ITERS, depth, OCTET, cells), f32),
            pltpu.VMEM((ITERS, OCTET, cells), f32),
            pltpu.VMEM((ITERS, OCTET, cells), f32),
            pltpu.VMEM((ITERS, group, OCTET, cells), f32),
            pltpu.VMEM((ITERS, group, OCTET, cells), f32),
            dma((6,)), pltpu.SemaphoreType.REGULAR((depth,)), dma, dma, dma((depth,)), dma((depth,)), dma, dma,
            dma, dma, dma((ITERS,)), dma((ITERS,)),
            dma, dma, dma((ITERS,)), dma((ITERS,)),
            dma((ITERS, depth)), dma((ITERS, depth)), dma((ITERS,)), dma((ITERS,)), dma((ITERS,)), dma((ITERS,)),
        ],
        compiler_params=pltpu.CompilerParams(collective_id=1, has_side_effects=True),
        name="parareal",
    )(initial_state, inv_mass[None], element_scale[None], mode_rate, volume_block, face_blocks)
    return (half_sum + half_difference)[None], (half_sum - half_difference)[None]


def solution(mesh):
    slices = mesh.shape["tm"]
    group = DOF // OCTET
    placed = (P(None, "space"), P("space"), P("space"), P("tm", None), P(), P())
    return jax.shard_map(
        functools.partial(per_device, slices // group, group),
        mesh=mesh,
        in_specs=placed,
        out_specs=(P("tm", None, "space"), P("tm", None, "space")),
        check_vma=False,
    )
```
